32 devices in a mesh: row: 8 (over z, y), col: 4 (over x, core).
Axes of the slice: x: 2, y: 2, z: 4, core: 2. Of those that a mesh axis runs over, the one named last changes fastest.
Arguments:
- spectra: bfloat16 [2, 2, 10240, 256], P(None, None, ('row', 'col')), may hold values from -40 to 40
- delays_s: int32 [10240, 512], P('row'), may hold values from 0 to 1023
- delays_r: int32 [10240, 512], P('col'), may hold values from 0 to 1023
- wl_index: int32 [2], replicated, may hold values from 0 to 10239
Outputs:
- beam_field: float32 [2, 2, 512, 512], P(None, None, 'col', 'row')
The draws below stay inside these ranges and needn't reach their ends.
All inputs are finite; a program needn't handle non-finite values.
Results may differ from the reference program's by a relative error of at most 0.0071.
Values may be sent and summed in bfloat16 or wider, within the bound.
No kernel may reach another device: no remote copies, remote signals or barrier semaphores. Data moves between devices by JAX's collectives and lax.ppermute only.
A program may use at most 128 MiB of HBM per device.

```python
import math
import jax
import jax.numpy as jnp
from jax import lax

FREQS = 2
STATIONS = 10240
WINDOWS = 256
BEAMS_R = 512
BEAMS_S = 512
N_ROW = 8
N_COL = 4


def draw_spectra(key, part):
    first, second = jax.random.split(key, 2)
    scales = jnp.exp(jax.random.uniform(second, (FREQS, 1, STATIONS, 1), jnp.float32, 0.0, math.log(10.0)))
    values = scales * jax.random.normal(first, (FREQS, 2, STATIONS, WINDOWS), jnp.float32)
    return jnp.clip(values, -40.0, 40.0).astype(jnp.bfloat16)


def touch_ends(entries, rng, smallest, largest):
    longest = entries.shape.index(max(entries.shape))
    spots = []
    for shift in (0, 1):
        where = [jax.random.randint(jax.random.fold_in(rng, axis), (), 0, length) for axis, length in enumerate(entries.shape)]
        where[longest] = (where[longest] + shift) % entries.shape[longest]
        spots.append(tuple(where))
    return entries.at[spots[0]].set(smallest).at[spots[1]].set(largest)


def setup_inputs(seed: int = 0) -> dict:
    key_of = jax.random.split(jax.random.key(seed), 5)
    spectra = draw_spectra(jax.random.fold_in(key_of[4], 71), 0)
    delays_s = touch_ends(jax.random.randint(key_of[1], (STATIONS, BEAMS_S), 0, 1024), jax.random.fold_in(key_of[1], 1), 0, 1023).astype(jnp.int32)
    delays_r = touch_ends(jax.random.randint(key_of[2], (STATIONS, BEAMS_R), 0, 1024), jax.random.fold_in(key_of[2], 1), 0, 1023).astype(jnp.int32)
    wl_index = jax.random.randint(key_of[3], (FREQS,), 0, STATIONS).astype(jnp.int32)
    return {"spectra": spectra, "delays_s": delays_s, "delays_r": delays_r, "wl_index": wl_index}


cycle_rates = (0.0361, 0.0596)
two_pi = 2.0 * math.pi

def steering(delays):
    rates = jnp.array(cycle_rates, jnp.float32)
    phase = (two_pi * rates)[:, None, None] * delays.astype(jnp.float32)[None]
    return (jnp.cos(phase).astype(jnp.bfloat16), jnp.sin(phase).astype(jnp.bfloat16))

def product(form, left, right):
    return jnp.einsum(form, left.astype(jnp.float32), right.astype(jnp.float32), precision=lax.Precision.HIGHEST)

def reference(spectra, delays_s, delays_r, wl_index):
    values = spectra.astype(jnp.float32)
    power = lax.optimization_barrier(jnp.sum(jnp.square(values), axis=(1, 3)))
    level = 0.5 * power[jnp.arange(FREQS, dtype=jnp.int32), wl_index]
    gain = lax.rsqrt(power + level[:, None])
    per_station = STATIONS // (N_ROW * N_COL)
    natural_r = delays_r.reshape(N_COL, N_ROW, per_station, BEAMS_R).transpose(1, 0, 2, 3).reshape(STATIONS, BEAMS_R)
    rec_cos, rec_sin = steering(natural_r)
    src_cos, src_sin = steering(delays_s)
    rec_cos = rec_cos.astype(jnp.float32)
    rec_sin = rec_sin.astype(jnp.float32)
    block = STATIONS // N_ROW

    def one_block(total, index):
        start = (index * block).astype(jnp.int32)
        rows = lax.dynamic_slice_in_dim(values, start, block, 2)
        row_gain = lax.dynamic_slice_in_dim(gain, start, block, 1)
        cross_re = product('fiw,fjw->fij', rows[:, 0], values[:, 0]) + product('fiw,fjw->fij', rows[:, 1], values[:, 1])
        cross_im = product('fiw,fjw->fij', rows[:, 1], values[:, 0]) - product('fiw,fjw->fij', rows[:, 0], values[:, 1])
        weight = row_gain[:, :, None] * gain[:, None, :]
        coh_re = lax.optimization_barrier((cross_re * weight).astype(jnp.bfloat16)).astype(jnp.float32)
        coh_im = lax.optimization_barrier((cross_im * weight).astype(jnp.bfloat16)).astype(jnp.float32)
        beam_re = product('fij,fjb->fib', coh_re, rec_cos) + product('fij,fjb->fib', coh_im, rec_sin)
        beam_im = product('fij,fjb->fib', coh_im, rec_cos) - product('fij,fjb->fib', coh_re, rec_sin)
        scos = lax.dynamic_slice_in_dim(src_cos, start, block, 1)
        ssin = lax.dynamic_slice_in_dim(src_sin, start, block, 1)
        out_re = product('fib,fia->fba', beam_re, scos) - product('fib,fia->fba', beam_im, ssin)
        out_im = product('fib,fia->fba', beam_im, scos) + product('fib,fia->fba', beam_re, ssin)
        return (total + jnp.stack([out_re, out_im], axis=1), None)
    empty = jnp.zeros((FREQS, 2, BEAMS_R, BEAMS_S), jnp.float32)
    total, _ = lax.scan(one_block, empty, jnp.arange(N_ROW, dtype=jnp.int32))
    return total * (math.sqrt(WINDOWS) / STATIONS)
```

```python
import math

import jax
import jax.numpy as jnp
from jax import lax
from jax.sharding import PartitionSpec as P

cycle_rates = (0.0361, 0.0596)
SIN = (3.141592502593994, -5.1677069664001465, 2.5500314235687256, -0.5980451703071594, 0.0772201269865036)
COS = (0.9999999403953552, -4.934792995452881, 4.058412075042725, -1.3318800926208496, 0.2196967601776123)


def horner(z, terms):
    total = terms[-1]
    for term in terms[-2::-1]:
        total = total * z + term
    return total


def steering(delays, rate):
    turns = rate * delays.astype(jnp.float32)
    turns = turns - jnp.round(turns)
    z = turns * turns
    half_sin = turns * horner(z, SIN)
    half_cos = horner(z, COS)
    sin = 2.0 * half_sin * half_cos
    cos = 1.0 - 2.0 * half_sin * half_sin
    return cos.astype(jnp.bfloat16), sin.astype(jnp.bfloat16)


def swap(value, axis, bit):
    size = lax.axis_size(axis)
    return lax.ppermute(value, axis, [(i, i ^ bit) for i in range(size)])


def pick(value, index, axis):
    return lax.dynamic_index_in_dim(value, index, axis, keepdims=False)


def pair(own, other, bit, axis=0):
    first = jnp.where(bit == 0, own, other)
    second = jnp.where(bit == 0, other, own)
    return jnp.stack([first, second], axis=axis)


def bits(size, start):
    found = []
    while start < size:
        found.append(start)
        start *= 2
    return found


def beams(spec, gain, cos, sin):
    scaled = (spec.astype(jnp.float32) * gain[..., None, :, None]).astype(jnp.bfloat16)
    real, imag = scaled[..., 0, :, :], scaled[..., 1, :, :]
    width = real.shape[-1]
    real, imag = real.reshape(-1, width), imag.reshape(-1, width)
    straight = jnp.concatenate([real, imag], axis=1)
    turned = jnp.concatenate([-imag, real], axis=1)
    return jnp.einsum("sb,sw->bw", cos, straight, preferred_element_type=jnp.float32) + jnp.einsum(
        "sb,sw->bw", sin, turned, preferred_element_type=jnp.float32
    )


def halve(value, axis, bit, at):
    other = swap(pick(value, 1 - at, 1).astype(jnp.bfloat16), axis, bit)
    return pick(value, at, 1) + other.astype(jnp.float32)


def add(value, axis, bit):
    mine = value.astype(jnp.bfloat16)
    return value + swap(mine, axis, bit).astype(jnp.float32)


def body(spectra, delays_s, delays_r, wl_index):
    n_row, n_col = lax.axis_size("row"), lax.axis_size("col")
    row, col = lax.axis_index("row"), lax.axis_index("col")
    per, windows = spectra.shape[2:]
    half = windows // 2
    core, x, y = col & 1, (col >> 1) & 1, row & 1

    power = jnp.sum(jnp.square(spectra.astype(jnp.float32)), axis=(1, 3))
    ids = (row * n_col + col) * per + jnp.arange(per, dtype=jnp.int32)
    picked = jnp.sum(jnp.where(ids[None, :] == wl_index[:, None], power, 0.0), axis=1)

    spec = pair(pick(spectra, core, 0), swap(pick(spectra, 1 - core, 0), "col", 1), core)
    note = jnp.concatenate([power, picked[:, None]], axis=1)
    note = pair(pick(note, core, 0), swap(pick(note, 1 - core, 0), "col", 1), core)
    power, level = note[:, :per], jnp.sum(note[:, per])

    halves = spec.reshape(*spec.shape[:-1], 2, half)
    spec_x = pair(pick(halves, x, 3), swap(pick(halves, 1 - x, 3), "col", 2), x)
    spec_y = pair(pick(halves, y, 3), swap(pick(halves, 1 - y, 3), "row", 1), y)

    note = jnp.concatenate([power.reshape(-1), level[None]])
    other = swap(note, "col", 2)
    power_x = pair(power, other[:-1].reshape(power.shape), x)
    level = level + other[-1]
    note = jnp.concatenate([power.reshape(-1), level[None]])
    other = swap(note, "row", 1)
    power_y = pair(power, other[:-1].reshape(power.shape), y)
    level = level + other[-1]
    for bit in bits(n_row, 2):
        level = level + swap(level[None], "row", bit)[0]
    for bit in bits(n_col, 4):
        level = level + swap(level[None], "col", bit)[0]
    level = 0.5 * level

    rate = jnp.where(core == 0, cycle_rates[0], cycle_rates[1]).astype(jnp.float32)
    beams_s, beams_r = delays_s.shape[1], delays_r.shape[1]
    near_s = pick(delays_s.reshape(n_col // 4, 4 * per, beams_s), col >> 2, 0)
    near_r = pick(delays_r.reshape(n_row // 2, 2 * per, beams_r), row >> 1, 0)
    near_r = pair(near_r, swap(near_r, "col", 1), core).reshape(4 * per, beams_r)
    src_cos, src_sin = steering(near_s, rate)
    rec_cos, rec_sin = steering(near_r, rate)

    source = beams(spec_x, lax.rsqrt(power_x + level), src_cos, src_sin)
    spec_y, power_y = spec_y.swapaxes(0, 1), power_y.swapaxes(0, 1)
    receiver = beams(spec_y, lax.rsqrt(power_y + level), rec_cos, rec_sin)

    for bit in bits(n_row, 1):
        source = source.reshape(n_row // (2 * bit), 2, -1, 2 * half)
        source = halve(source, "row", bit, (row // bit) & 1)
    source = source.reshape(-1, 2 * half)
    for bit in bits(n_col, 4):
        source = add(source, "col", bit)
    source = source.astype(jnp.bfloat16)
    source = pair(source, swap(source, "col", 2), x)

    for bit in bits(n_col, 2):
        receiver = receiver.reshape(n_col // (2 * bit), 2, -1, 2 * half)
        receiver = halve(receiver, "col", bit, (col // bit) & 1)
    receiver = receiver.reshape(-1, 2 * half)
    for bit in bits(n_row, 2):
        receiver = add(receiver, "row", bit)
    receiver = receiver.astype(jnp.bfloat16)
    receiver = pair(receiver, swap(receiver, "row", 1), y)

    def joined(left, right):
        return jnp.einsum("hbw,haw->ba", left, right, preferred_element_type=jnp.float32)

    s_re, s_im = source[..., :half], source[..., half:]
    r_re, r_im = receiver[..., :half], receiver[..., half:]
    field = jnp.stack(
        [joined(r_re, s_re) + joined(r_im, s_im), joined(r_re, s_im) - joined(r_im, s_re)], axis=0
    )
    field = field * (math.sqrt(windows) / (per * n_row * n_col))
    field = field.reshape(2, 2, -1, field.shape[-1])
    return pair(pick(field, core, 1), swap(pick(field, 1 - core, 1), "col", 1), core)


def solution(mesh):
    in_specs = (P(None, None, ("row", "col"), None), P("row", None), P("col", None), P())
    out_specs = P(None, None, "col", "row")
    return jax.shard_map(body, mesh=mesh, in_specs=in_specs, out_specs=out_specs, check_vma=False)
```

```python
import functools
import math

import jax
import jax.numpy as jnp
from jax import lax
from jax.experimental import pallas as pl
from jax.experimental.pallas import tpu as pltpu
from jax.sharding import PartitionSpec as P

cycle_rates = (0.0361, 0.0596)
ROOT = math.sqrt(2.0)
SIN = (3.1415820121765137, -5.167142868041992, 2.5418989658355713, -0.5546361207962036)
COS = (0.9999999403953552, -4.934792995452881, 4.058412075042725, -1.3318800926208496, 0.2196967601776123)


def horner(z, terms):
    total = ROOT * terms[-1]
    for term in terms[-2::-1]:
        total = total * z + ROOT * term
    return total


def steer_rows(rate, delays):
    turns = rate * delays.astype(jnp.float32)
    turns = turns - jnp.round(turns)
    z = turns * turns
    half_sin = turns * horner(z, SIN)
    half_cos = horner(z, COS)
    return (1.0 - half_sin * half_sin).astype(jnp.bfloat16), (half_sin * half_cos).astype(jnp.bfloat16)


CHUNK = 32
LANES = 128


def place():
    row, col = lax.axis_index("row"), lax.axis_index("col")
    return row, col, col & 1, (col >> 1) & 1, row & 1


def y_of():
    return place()[4]


def block_of(j, at):
    _, col, core, x, _ = place()
    return (col >> 2) * 4 + (x ^ j) * 2 + (core ^ at)


def vmem(shape, dtype):
    return pltpu.VMEM(shape, dtype)


def kernel_call(body, out, inputs, spaces, scratch=(), limit=8, cost=1):
    held = [
        pltpu.with_memory_space_constraint(v, space) if space in (pltpu.HBM, pltpu.VMEM) else v
        for v, space in zip(inputs, spaces)
    ]
    return pl.pallas_call(
        body,
        out_shape=out,
        in_specs=[pl.BlockSpec(memory_space=space) for space in spaces],
        out_specs=[pl.BlockSpec(memory_space=pltpu.VMEM)] * len(out),
        scratch_shapes=list(scratch),
        compiler_params=pltpu.CompilerParams(vmem_limit_bytes=limit * 2**20),
        cost_estimate=pl.CostEstimate(flops=1, bytes_accessed=cost, transcendentals=0),
    )(*held)


def power_kernel(wl_ref, spec_ref, note_ref, held_ref, wl_held, sems):
    row, col, *_ = place()
    n_col = lax.axis_size("col")
    freqs, _, per, windows = spec_ref.shape
    wl_copy = pltpu.make_async_copy(wl_ref, wl_held, sems.at[freqs])
    copies = [pltpu.make_async_copy(spec_ref.at[f], held_ref.at[f], sems.at[f]) for f in range(freqs)]
    wl_copy.start()
    for copy in copies:
        copy.start()
    note_ref[...] = jnp.zeros_like(note_ref)
    ids = (row * n_col + col) * per + lax.broadcasted_iota(jnp.int32, (1, per), 1)
    rest = jnp.zeros((note_ref.shape[2] - per, LANES), jnp.float32)
    wl_copy.wait()
    for f, copy in enumerate(copies):
        copy.wait()
        squares = jnp.square(held_ref[f].astype(jnp.float32))
        squares = squares[0] + squares[1]
        squares = sum(squares[:, at : at + LANES] for at in range(0, windows, LANES))
        columns = jnp.transpose(jnp.concatenate([squares, rest], axis=0))
        power = jnp.sum(columns, axis=0, keepdims=True)[:, :per]
        level = jnp.sum(jnp.where(ids == wl_held[f], power, 0.0), axis=1, keepdims=True)
        note_ref[f, 0:1, :per] = power
        note_ref[f, 1:2, :] = jnp.broadcast_to(level, (1, note_ref.shape[2]))


def gate_kernel(n, *refs):
    out_ref, start = refs[-1], 0
    for ref in refs[:n]:
        out_ref[start : start + ref.shape[0], :] = ref[...]
        start += ref.shape[0]


def gated(values, others):
    rows, width = sum(v.shape[0] for v in values), values[0].shape[1]
    return kernel_call(
        functools.partial(gate_kernel, len(values)),
        [vmem((rows, width), values[0].dtype)],
        [*values, *others],
        [pltpu.VMEM] * (len(values) + len(others)),
    )[0]


def steer_blocks(blocks, delays_ref, cos_ref, sin_ref):
    core = place()[2]
    rate = jnp.where(core == 0, cycle_rates[0], cycle_rates[1]).astype(jnp.float32)
    size = cos_ref.shape[0] // len(blocks)
    chunk = math.gcd(CHUNK, size)
    for index, (start, copy) in enumerate(blocks):
        if copy is not None:
            copy.wait()

        @pl.loop(0, size // chunk)
        def _(i):
            here = pl.ds(pl.multiple_of(start + i * chunk, chunk), chunk)
            there = pl.ds(pl.multiple_of(index * size + i * chunk, chunk), chunk)
            cos, sin = steer_rows(rate, delays_ref[here, :])
            cos_ref[there, :] = cos
            sin_ref[there, :] = sin


def steer_kernel(starts, token_ref, delays_ref, cos_ref, sin_ref):
    steer_blocks([(start, None) for start in starts(delays_ref.shape[0])], delays_ref, cos_ref, sin_ref)


def steer_far_kernel(parts, token_ref, delays_ref, cos_ref, sin_ref, held_ref, sems):
    row, *_, y = place()
    per = cos_ref.shape[0] // 2
    rows = per // parts
    blocks = []
    for index in range(2 * parts):
        j, part = divmod(index, parts)
        start = pl.multiple_of((row ^ j) * per + part * rows, 8)
        here = pl.ds(index * rows, rows)
        copy = pltpu.make_async_copy(delays_ref.at[pl.ds(start, rows), :], held_ref.at[here, :], sems.at[index])
        copy.start()
        blocks.append((index * rows, copy))
    steer_blocks(blocks, held_ref, cos_ref, sin_ref)


def steering(starts, rows, token, delays):
    out = [vmem((rows, delays.shape[1]), jnp.bfloat16)] * 2
    return kernel_call(functools.partial(steer_kernel, starts), out, [token, delays], [pltpu.VMEM] * 2)


def steering_far(rows, token, delays):
    width = delays.shape[1]
    parts = math.gcd(rows // (2 * CHUNK), 5)
    return kernel_call(
        functools.partial(steer_far_kernel, parts),
        [vmem((rows, width), jnp.bfloat16)] * 2,
        [token, delays],
        [pltpu.VMEM, pltpu.HBM],
        scratch=[pltpu.VMEM((rows, width), delays.dtype), pltpu.SemaphoreType.DMA((2 * parts,))],
    )


def beams_kernel(axis, order, near_power_ref, far_ref, level_ref, near_ref, from_ref, *refs):
    *steer, out_ref = refs
    per, half = from_ref.shape[2:]
    _, _, _, x, y = place()
    mine = pl.ds(pl.multiple_of((x if axis == "x" else y) * half, half), half)
    level = 0.5 * level_ref[...]
    real, imag = [], []
    for at in range(4):
        power = near_power_ref[at : at + 1] if at < 2 else far_ref[at - 2 : at - 1]
        gain = jnp.transpose(jnp.broadcast_to(lax.rsqrt(power + level), (8, level.shape[1])))[:per, :1]
        for part, parts in enumerate((real, imag)):
            spec = near_ref[at, part, :, mine] if at < 2 else from_ref[at - 2, part]
            parts.append(spec.astype(jnp.float32) * gain)
    total = None
    count = len(steer) // 2
    for group in range(count):
        members = order[group * 4 // count : (group + 1) * 4 // count]
        re, im = (jnp.concatenate([p[m] for m in members], axis=0).astype(jnp.bfloat16) for p in (real, imag))
        for left, right in (((re, im), steer[2 * group]), ((-im, re), steer[2 * group + 1])):
            term = lax.dot_general(
                right[...],
                jnp.concatenate(left, axis=1),
                (((0,), (0,)), ((), ())),
                preferred_element_type=jnp.float32,
            )
            total = term if total is None else total + term
    out_ref[...] = total


def beams(axis, order, near_power, far, level, near, arrived, steer):
    inputs = [near_power, far, level, near, arrived, *steer]
    out = [vmem((steer[0].shape[1], 2 * arrived.shape[-1]), jnp.float32)]
    return kernel_call(functools.partial(beams_kernel, axis, order), out, inputs, [pltpu.VMEM] * len(inputs), limit=24)[0]


def swap(value, axis, bit):
    size = lax.axis_size(axis)
    return lax.ppermute(value, axis, [(i, i ^ bit) for i in range(size)])


def choose(bit, first, second):
    return jnp.where(bit == 0, first, second)


def ordered(bit, own, other):
    return choose(bit, own, other), choose(bit, other, own)


def bits(size, start):
    found = []
    while start < size:
        found.append(start)
        start *= 2
    return found


tie = lax.optimization_barrier


def halve(value, dim, axis, bit, at):
    first, second = lax.index_in_dim(value, 0, dim, False), lax.index_in_dim(value, 1, dim, False)
    return choose(at, first, second), swap(choose(at, second, first).astype(jnp.bfloat16), axis, bit)


def total(parts):
    own, other = parts
    return own + other.astype(jnp.float32)


def body(spectra, delays_s, delays_r, wl_index):
    n_row, n_col = lax.axis_size("row"), lax.axis_size("col")
    row, col, core, x, y = place()
    per, windows = spectra.shape[2:]
    half = windows // 2
    core, x, y = col & 1, (col >> 1) & 1, row & 1
    beams_r = delays_r.shape[1]

    partner = swap(spectra, "col", 1)
    freqs, padded = spectra.shape[0], -(-per // LANES) * LANES
    (note,) = kernel_call(
        power_kernel,
        [vmem((freqs, 2, padded), jnp.float32)],
        [wl_index, spectra],
        [pltpu.HBM, pltpu.HBM],
        scratch=[
            pltpu.VMEM(spectra.shape, spectra.dtype),
            pltpu.SMEM(wl_index.shape, wl_index.dtype),
            pltpu.SemaphoreType.DMA((freqs + 1,)),
        ],
        cost=2 * spectra.size * 2,
    )
    other = swap(note, "col", 1)
    note, other = choose(core, note[0], note[1]), choose(core, other[0], other[1])
    power = jnp.concatenate([note[:1], other[:1]])
    level = note[1:] + other[1:]

    spec = jnp.stack([choose(core, spectra[0], spectra[1]), choose(core, partner[0], partner[1])])
    low, high = spec[..., :half], spec[..., half:]
    from_x, from_y = swap(choose(x, high, low), "col", 2), swap(choose(y, high, low), "row", 1)

    near_r = lax.dynamic_slice_in_dim(delays_r, (row >> 1) * (2 * per), 2 * per, 0)
    other_r = swap(near_r.astype(jnp.int16), "col", 1)
    row_bits, col_bits = bits(n_row, 2), bits(n_col, 4)
    for bit in row_bits[:1]:
        level = level + swap(level, "row", bit)
    steer_r = steering_far(2 * per, level, delays_r)
    steer_r += steering(lambda rows: [(y_of() ^ j) * (rows // 2) for j in (0, 1)], 2 * per, level, other_r)
    for bit in row_bits[1:]:
        level = level + swap(level, "row", bit)
    for bit in col_bits:
        level = level + swap(level, "col", bit)
    steer_s = steering(lambda rows: [block_of(0, at) * per for at in (0, 1)], 2 * per, level, delays_s)
    far_x = swap(gated([power, level], [from_x, from_y]), "col", 2)
    level = level + far_x[2:]
    steer_s += steering(lambda rows: [block_of(1, at) * per for at in (0, 1)], 2 * per, level, delays_s)
    far_y = swap(jnp.concatenate([power, level]), "row", 1)
    level = level + far_y[2:]

    receiver = beams("y", (0, 2, 1, 3), power, far_y, level, spec, from_y, steer_r)
    source = beams("x", (0, 1, 2, 3), power, far_x, level, spec, from_x, steer_s)

    row_bits, col_bits = bits(n_row, 1), bits(n_col, 2)
    receiver = receiver.reshape((2,) * len(col_bits) + (-1, 2 * half))
    source = source.reshape((2,) * len(row_bits) + (-1, 2 * half))

    def scatter(axis, bit, dim):
        index = row if axis == "row" else col
        return (lambda v: halve(v, dim, axis, bit, (index // bit) & 1)), total

    def add(axis, bit):
        return (lambda v: (v, swap(v.astype(jnp.bfloat16), axis, bit))), total

    def gather(axis, bit, index):
        def send(v):
            v = v.astype(jnp.bfloat16)
            return v, swap(v, axis, bit)

        return send, lambda parts: jnp.stack(ordered(index, *parts), axis=-3)

    receiver_steps = [scatter("col", bit, 0) for bit in col_bits[::-1]]
    receiver_steps += [add("row", bit) for bit in row_bits[1:]] + [gather("row", 1, y)]
    source_steps = [scatter("row", 2, len(row_bits) - 2), scatter("row", 1, -3), gather("col", 2, x)]
    source_steps += [scatter("row", bit, 0) for bit in row_bits[:1:-1]]
    source_steps += [add("col", bit) for bit in col_bits[1:]]
    for index in range(max(len(receiver_steps), len(source_steps))):
        sent = []
        if index < len(receiver_steps):
            sent.append(receiver_steps[index][0](receiver))
        if index < len(source_steps):
            sent.append(source_steps[index][0](source))
        sent = tie(sent)
        if index < len(receiver_steps):
            receiver = receiver_steps[index][1](sent[0])
        if index < len(source_steps):
            source = source_steps[index][1](sent[-1])
    receiver, source = receiver.astype(jnp.bfloat16), source.astype(jnp.bfloat16)

    def flat(parts):
        return jnp.concatenate(parts, axis=1)

    left, real = flat(receiver), flat(source)
    imag = flat([v for s in source for v in (s[:, half:], -s[:, :half])])
    field = jnp.stack(
        [jnp.dot(left, right.T, preferred_element_type=jnp.float32) for right in (real, imag)]
    )
    field = field * (math.sqrt(windows) / (per * n_row * n_col))
    field = field.reshape(2, 2, -1, field.shape[-1])
    first, second = field[:, 0], field[:, 1]
    return jnp.stack(ordered(core, choose(core, first, second), swap(choose(core, second, first), "col", 1)))


def solution(mesh):
    in_specs = (P(None, None, ("row", "col"), None), P("row", None), P("col", None), P())
    out_specs = P(None, None, "col", "row")
    return jax.shard_map(body, mesh=mesh, in_specs=in_specs, out_specs=out_specs, check_vma=False)
```

```python
import functools
import math

import jax
import jax.numpy as jnp
from jax import lax
from jax.experimental import pallas as pl
from jax.experimental.pallas import tpu as pltpu
from jax.sharding import PartitionSpec as P

cycle_rates = (0.0361, 0.0596)
ROOT = math.sqrt(2.0)
SIN = (3.1415820121765137, -5.167142868041992, 2.5418989658355713, -0.5546361207962036)
COS = (0.9999999403953552, -4.934792995452881, 4.058412075042725, -1.3318800926208496, 0.2196967601776123)


def horner(z, terms):
    total = ROOT * terms[-1]
    for term in terms[-2::-1]:
        total = total * z + ROOT * term
    return total


def steer_rows(rate, delays):
    turns = rate * delays.astype(jnp.float32)
    turns = turns - jnp.round(turns)
    z = turns * turns
    half_sin = turns * horner(z, SIN)
    half_cos = horner(z, COS)
    return (1.0 - half_sin * half_sin).astype(jnp.bfloat16), (half_sin * half_cos).astype(jnp.bfloat16)


CHUNK = 32
LANES = 128


def place():
    row, col = lax.axis_index("row"), lax.axis_index("col")
    return row, col, col & 1, (col >> 1) & 1, row & 1


def y_of():
    return place()[4]


def block_of(j, at):
    _, col, core, x, _ = place()
    return (col >> 2) * 4 + (x ^ j) * 2 + (core ^ at)


def vmem(shape, dtype):
    return pltpu.VMEM(shape, dtype)


def kernel_call(body, out, inputs, spaces, scratch=(), limit=8, cost=1, name=None):
    held = [
        pltpu.with_memory_space_constraint(v, space) if space in (pltpu.HBM, pltpu.VMEM) else v
        for v, space in zip(inputs, spaces)
    ]
    return pl.pallas_call(
        body,
        out_shape=out,
        in_specs=[pl.BlockSpec(memory_space=space) for space in spaces],
        out_specs=[pl.BlockSpec(memory_space=pltpu.VMEM)] * len(out),
        scratch_shapes=list(scratch),
        compiler_params=pltpu.CompilerParams(vmem_limit_bytes=limit * 2**20),
        cost_estimate=pl.CostEstimate(flops=1, bytes_accessed=cost, transcendentals=0),
        name=name,
    )(*held)


def power_kernel(wl_ref, spec_ref, own_note, away_note, own_ref, away_ref, wl_held, sems):
    row, col, core, *_ = place()
    n_col = lax.axis_size("col")
    _, parts, per, windows = spec_ref.shape
    wl_copy = pltpu.make_async_copy(wl_ref, wl_held, sems.at[2])
    wl_copy.start()
    both = ((core, own_note, own_ref), (1 - core, away_note, away_ref))
    copies = [pltpu.make_async_copy(spec_ref.at[f], held, sems.at[i]) for i, (f, _, held) in enumerate(both)]
    for copy in copies:
        copy.start()
    ids = (row * n_col + col) * per + lax.broadcasted_iota(jnp.int32, (1, per), 1)
    rest = jnp.zeros((own_note.shape[1] - per, LANES), jnp.float32)
    wl_copy.wait()
    for (f, note, held), copy in zip(both, copies):
        copy.wait()
        squares = jnp.square(held[...].astype(jnp.float32))
        squares = squares[0] + squares[1]
        squares = sum(squares[:, at : at + LANES] for at in range(0, windows, LANES))
        columns = jnp.transpose(jnp.concatenate([squares, rest], axis=0))
        power = jnp.sum(columns, axis=0, keepdims=True)
        level = jnp.sum(jnp.where(ids == wl_held[f], power[:, :per], 0.0), axis=1, keepdims=True)
        note[0:1, :] = power
        note[1:2, :] = jnp.broadcast_to(level, power.shape)


def gate_kernel(n, *refs):
    out_ref, start = refs[-1], 0
    for ref in refs[:n]:
        out_ref[start : start + ref.shape[0], :] = ref[...]
        start += ref.shape[0]


def gated(values, others):
    rows, width = sum(v.shape[0] for v in values), values[0].shape[1]
    return kernel_call(
        functools.partial(gate_kernel, len(values)),
        [vmem((rows, width), values[0].dtype)],
        [*values, *others],
        [pltpu.VMEM] * (len(values) + len(others)),
        name="gate",
    )[0]


def send_kernel(token_ref, own_ref, other_ref, to_x_ref, to_y_ref):
    y = place()[4]
    half = to_y_ref.shape[-1]
    theirs = pl.ds(pl.multiple_of((1 - y) * half, half), half)
    for at, ref in enumerate((own_ref, other_ref)):
        to_x_ref[at] = ref[...]
        for part in range(ref.shape[0]):
            to_y_ref[at, part] = ref[part, :, theirs]


def steer_blocks(blocks, delays_ref, cos_ref, sin_ref, copy_ref=None):
    core = place()[2]
    rate = jnp.where(core == 0, cycle_rates[0], cycle_rates[1]).astype(jnp.float32)
    size = cos_ref.shape[0] // len(blocks)
    chunk = math.gcd(CHUNK, size)
    for index, (start, arrival) in enumerate(blocks):
        if arrival is not None:
            arrival.wait()

        @pl.loop(0, size // chunk)
        def _(i):
            here = pl.ds(pl.multiple_of(start + i * chunk, chunk), chunk)
            there = pl.ds(pl.multiple_of(index * size + i * chunk, chunk), chunk)
            delays = delays_ref[here, :]
            cos, sin = steer_rows(rate, delays)
            cos_ref[there, :] = cos
            sin_ref[there, :] = sin
            if copy_ref is not None:
                copy_ref[there, :] = delays.astype(copy_ref.dtype)


def steer_kernel(token_ref, delays_ref, cos_ref, sin_ref, out_ref):
    out_ref[...] = token_ref[...]
    steer_blocks([(0, None)], delays_ref, cos_ref, sin_ref)


def steer_far_kernel(starts, parts, token_ref, delays_ref, cos_ref, sin_ref, out_ref, *refs):
    *copy_ref, held_ref, sems = refs
    out_ref[...] = token_ref[...]
    per = cos_ref.shape[0] // 2
    rows = per // parts
    blocks = []
    for j, first in enumerate(starts()):
        for part in range(parts):
            index = j * parts + part
            here = pl.ds(index * rows, rows)
            there = pl.ds(pl.multiple_of(first + part * rows, 8), rows)
            arrival = pltpu.make_async_copy(delays_ref.at[there, :], held_ref.at[here, :], sems.at[index])
            arrival.start()
            blocks.append((index * rows, arrival))
    steer_blocks(blocks, held_ref, cos_ref, sin_ref, *copy_ref)


def steering(token, delays):
    out = [vmem(delays.shape, jnp.bfloat16)] * 2 + [vmem(token.shape, token.dtype)]
    return kernel_call(steer_kernel, out, [token, delays], [pltpu.VMEM] * 2, name="steering")


def steering_far(starts, rows, token, delays, copied=()):
    width = delays.shape[1]
    parts = math.gcd(rows // (2 * CHUNK), 5)
    return kernel_call(
        functools.partial(steer_far_kernel, starts, parts),
        [vmem((rows, width), jnp.bfloat16)] * 2
        + [vmem(token.shape, token.dtype)]
        + [vmem((rows, width), t) for t in copied],
        [token, delays],
        [pltpu.VMEM, pltpu.HBM],
        scratch=[pltpu.VMEM((rows, width), delays.dtype), pltpu.SemaphoreType.DMA((2 * parts,))],
        name="steering_far",
    )


def halves(total, block, bit, keep_ref, send_ref):
    for pair in range(keep_ref.shape[0] // block):
        out = pl.ds(pair * block, block)
        for ref, at in ((keep_ref, bit), (send_ref, 1 - bit)):
            rows = pl.ds(pl.multiple_of((2 * pair + at) * block, block), block)
            ref[out, :] = total[rows, :].astype(ref.dtype)


def beams_kernel(order, mine, block, kept, near_power_ref, far_ref, level_ref, own_ref, other_ref, from_ref, *refs):
    *steer, keep_ref, send_ref, token_ref, total_ref = refs
    token_ref[...] = level_ref[...]
    per = from_ref.shape[2]
    windows = mine(from_ref.shape[3])
    level = 0.5 * level_ref[...]
    real, imag = [], []
    for at in range(4):
        power = near_power_ref[at : at + 1] if at < 2 else far_ref[at - 2 : at - 1]
        gain = jnp.transpose(jnp.broadcast_to(lax.rsqrt(power + level), (8, level.shape[1])))[:per, :1]
        for part, parts in enumerate((real, imag)):
            near_ref = (own_ref, other_ref)[at % 2]
            spec = near_ref[part, :, windows] if at < 2 else from_ref[at - 2, part]
            parts.append(spec.astype(jnp.float32) * gain)
    total = None
    count = len(steer) // 2
    for group in range(count):
        members = order[group * 4 // count : (group + 1) * 4 // count]
        re, im = (jnp.concatenate([p[m] for m in members], axis=0).astype(jnp.bfloat16) for p in (real, imag))
        for left, right in (((re, im), steer[2 * group]), ((-im, re), steer[2 * group + 1])):
            term = lax.dot_general(
                right[...],
                jnp.concatenate(left, axis=1),
                (((0,), (0,)), ((), ())),
                preferred_element_type=jnp.float32,
            )
            total = term if total is None else total + term
    total_ref[...] = total
    halves(total_ref, block, kept(), keep_ref, send_ref)


def beams(order, mine, block, kept, near_power, far, level, own, other, arrived, steer, name):
    inputs = [near_power, far, level, own, other, arrived, *steer]
    rows, width = steer[0].shape[1], 2 * arrived.shape[-1]
    return kernel_call(
        functools.partial(beams_kernel, order, mine, block, kept),
        [
            vmem((rows // 2, width), jnp.float32),
            vmem((rows // 2, width), jnp.bfloat16),
            vmem(level.shape, level.dtype),
        ],
        inputs,
        [pltpu.VMEM] * len(inputs),
        scratch=[pltpu.VMEM((rows, width), jnp.float32)],
        limit=24,
        name=name,
    )


def step_kernel(block, axis, bit, given, keep_ref, other_ref, token_ref, *outs):
    if given:
        *outs, out_token_ref = outs if bit is None else (*outs[:2], outs[3], outs[2])
        out_token_ref[...] = token_ref[...]
    if bit is None:
        total = keep_ref[...] + other_ref[...].astype(jnp.float32)
        for ref in outs:
            ref[...] = total.astype(ref.dtype)
    else:
        keep_out, send_out, total_ref = outs
        total_ref[...] = keep_ref[...] + other_ref[...].astype(jnp.float32)
        index = lax.axis_index(axis)
        halves(total_ref, block, (index // bit) & 1, keep_out, send_out)


def exchange(keep, send, block, steps, given, name):
    token = yield
    for index, (axis, bit, _) in enumerate(steps):
        other = swap(send, axis, bit)
        rows, width = keep.shape
        scratch, cut = [], (None, None)
        if index + 1 == len(steps):
            out = [vmem((rows, width), jnp.bfloat16)]
        elif steps[index + 1][2]:
            out, cut = [vmem((rows // 2, width), t) for t in (jnp.float32, jnp.bfloat16)], steps[index + 1][:2]
            scratch = [pltpu.VMEM((rows, width), jnp.float32)]
        else:
            out = [vmem((rows, width), t) for t in (jnp.float32, jnp.bfloat16)]
        if index in given:
            out.append(vmem(token.shape, token.dtype))
        results = kernel_call(
            functools.partial(step_kernel, block, *cut, index in given),
            out,
            [keep, other, token],
            [pltpu.VMEM] * 3,
            scratch=scratch,
            name=name,
        )
        if index + 1 == len(steps):
            yield results[0]
        else:
            keep, send = results[:2]
            token = yield results[-1]


def field_kernel(scale, source_ref, near_r, far_r, keep_ref, send_ref):
    _, _, core, _, y = place()
    half = near_r.shape[1] // 2
    block = keep_ref.shape[2]

    def product(left, right):
        return lax.dot_general(left, right, (((1,), (1,)), ((), ())), preferred_element_type=jnp.float32)

    for ref, at in ((keep_ref, core), (send_ref, 1 - core)):
        rows = pl.ds(pl.multiple_of(at * block, block), block)
        real = imag = 0.0
        for bit, receiver in ((y, near_r), (1 - y, far_r)):
            s_re, s_im = (
                source_ref[:, pl.ds(pl.multiple_of((2 * part + bit) * half, half), half)] for part in (0, 1)
            )
            r_re, r_im = receiver[rows, :half], receiver[rows, half:]
            real += product(s_re, r_re) + product(s_im, r_im)
            imag += product(s_im, r_re) - product(s_re, r_im)
        ref[0] = real * scale
        ref[1] = imag * scale


def swap(value, axis, bit):
    size = lax.axis_size(axis)
    return lax.ppermute(value, axis, [(i, i ^ bit) for i in range(size)])


def choose(bit, first, second):
    return jnp.where(bit == 0, first, second)


def ordered(bit, own, other):
    return choose(bit, own, other), choose(bit, other, own)


def bits(size, start):
    found = []
    while start < size:
        found.append(start)
        start *= 2
    return found


def body(spectra, delays_s, delays_r, wl_index):
    n_row, n_col = lax.axis_size("row"), lax.axis_size("col")
    row, col, core, x, y = place()
    freqs, parts, per, windows = spectra.shape
    half = windows // 2
    padded = -(-per // LANES) * LANES

    spec_shape, note_shape = vmem((parts, per, windows), spectra.dtype), vmem((2, padded), jnp.float32)
    note, away_note, own, away = kernel_call(
        power_kernel,
        [note_shape, note_shape, spec_shape, spec_shape],
        [wl_index, spectra],
        [pltpu.HBM, pltpu.HBM],
        scratch=[pltpu.SMEM(wl_index.shape, wl_index.dtype), pltpu.SemaphoreType.DMA((3,))],
        name="power",
    )
    other_note, other = swap(away_note, "col", 1), swap(away, "col", 1)
    power = jnp.concatenate([note[:1], other_note[:1]])
    level = note[1:] + other_note[1:]

    def rows_r():
        return [(place()[0] ^ j) * per for j in (0, 1)]

    def rows_s(j):
        return lambda: [block_of(j, at) * per for at in (0, 1)]

    far_x = swap(jnp.concatenate([power, level]), "col", 2)
    *steer_r, token, near_r = steering_far(rows_r, 2 * per, note[1:], delays_r, [jnp.int16])
    other_r = swap(near_r, "col", 1)
    level = gated([level + far_x[2:]], [token])

    sent = [vmem((2, parts, per, w), spectra.dtype) for w in (windows, half)]
    to_x, to_y = kernel_call(send_kernel, sent, [level, own, other], [pltpu.VMEM] * 3, name="send")
    from_x, from_y = swap(to_x, "col", 2), swap(to_y, "row", 1)

    row_bits, col_bits = bits(n_row, 2), bits(n_col, 4)
    *steer_s, token = steering_far(rows_s(0), 2 * per, level, delays_s)
    first, *others = [("row", bit) for bit in row_bits] + [("col", bit) for bit in col_bits]
    level = level + swap(level, *first)
    cos, sin, next_token = steering_far(rows_s(1), 2 * per, level, delays_s)
    steer_s += [cos, sin]
    for step in others:
        level = gated([level], [token])
        level = level + swap(level, *step)
    cos, sin, token = steering(level, other_r)
    steer_r += [cos, sin]
    far_y = swap(gated([power, level], [from_y, next_token]), "row", 1)
    level = gated([level + far_y[2:]], [token])

    block_r, block_s = 2 * delays_r.shape[1] // n_col, delays_s.shape[1] // n_row
    keep_r, send_r, token = beams(
        (0, 2, 1, 3),
        lambda half: pl.ds(pl.multiple_of(y_of() * half, half), half),
        block_r,
        lambda: place()[3],
        power,
        far_y,
        level,
        own,
        other,
        from_y,
        steer_r,
        "beams_r",
    )
    keep_s, send_s, _ = beams(
        (0, 1, 2, 3), lambda windows: slice(None), block_s, y_of, power, far_x, token, own, other, from_x, steer_s, "beams_s"
    )
    r_steps = [("col", bit, True) for bit in [2, *col_bits]] + [("row", bit, False) for bit in row_bits]
    s_steps = [("row", bit, True) for bit in [1, *row_bits]] + [("col", bit, False) for bit in col_bits]
    late = 1
    r_chain = exchange(keep_r, send_r, block_r, r_steps, (), "step_r")
    s_chain = exchange(keep_s, send_s, block_s, s_steps, (late - 1,), "step_s")
    next(r_chain), next(s_chain)
    token = level
    for index in range(max(len(r_steps), len(s_steps))):
        if index < len(r_steps):
            receiver = r_chain.send(token if index == late else level)
        if index < len(s_steps):
            source = s_chain.send(level)
            if index == late - 1:
                token = source
    r_far = swap(receiver, "row", 1)

    block = delays_r.shape[1] // n_col
    shape = vmem((2, block_s, block), jnp.float32)
    scale = math.sqrt(windows) / (per * n_row * n_col)
    near, away = kernel_call(
        functools.partial(field_kernel, scale),
        [shape, shape],
        [source, receiver, r_far],
        [pltpu.VMEM] * 3,
        name="field",
    )
    far = swap(away, "col", 1)
    return jnp.stack(ordered(core, near, far)).swapaxes(2, 3)


def solution(mesh):
    in_specs = (P(None, None, ("row", "col"), None), P("row", None), P("col", None), P())
    out_specs = P(None, None, "col", "row")
    return jax.shard_map(body, mesh=mesh, in_specs=in_specs, out_specs=out_specs, check_vma=False)
```

```python
import functools
import math

import jax
import jax.numpy as jnp
from jax import lax
from jax.experimental import pallas as pl
from jax.experimental.pallas import tpu as pltpu
from jax.sharding import PartitionSpec as P

cycle_rates = (0.0361, 0.0596)
ROOT = math.sqrt(2.0)
SIN = (3.1415820121765137, -5.167142868041992, 2.5418989658355713, -0.5546361207962036)
COS = (0.9999999403953552, -4.934792995452881, 4.058412075042725, -1.3318800926208496, 0.2196967601776123)


def horner(z, terms):
    total = ROOT * terms[-1]
    for term in terms[-2::-1]:
        total = total * z + ROOT * term
    return total


def steer_rows(rate, delays):
    turns = rate * delays.astype(jnp.float32)
    turns = turns - jnp.round(turns)
    z = turns * turns
    half_sin = turns * horner(z, SIN)
    half_cos = horner(z, COS)
    return (1.0 - half_sin * half_sin).astype(jnp.bfloat16), (half_sin * half_cos).astype(jnp.bfloat16)


CHUNK = 32
LANES = 128


def place():
    row, col = lax.axis_index("row"), lax.axis_index("col")
    return row, col, col & 1, (col >> 1) & 1, row & 1


def y_of():
    return place()[4]


def block_of(j, at):
    _, col, core, x, _ = place()
    return (col >> 2) * 4 + (x ^ j) * 2 + (core ^ at)


def vmem(shape, dtype):
    return pltpu.VMEM(shape, dtype)


def kernel_call(body, out, inputs, spaces, scratch=(), limit=8, cost=1, name=None):
    held = [
        pltpu.with_memory_space_constraint(v, space) if space in (pltpu.HBM, pltpu.VMEM) else v
        for v, space in zip(inputs, spaces)
    ]
    return pl.pallas_call(
        body,
        out_shape=out,
        in_specs=[pl.BlockSpec(memory_space=space) for space in spaces],
        out_specs=[pl.BlockSpec(memory_space=pltpu.VMEM)] * len(out),
        scratch_shapes=list(scratch),
        compiler_params=pltpu.CompilerParams(vmem_limit_bytes=limit * 2**20),
        cost_estimate=pl.CostEstimate(flops=1, bytes_accessed=cost, transcendentals=0),
        name=name,
    )(*held)


def power_kernel(wl_ref, spec_ref, notes_ref, own_ref, away_ref, wl_held, sems):
    row, col, core, *_ = place()
    n_col = lax.axis_size("col")
    _, parts, per, windows = spec_ref.shape
    wl_copy = pltpu.make_async_copy(wl_ref, wl_held, sems.at[2])
    wl_copy.start()
    both = ((core, own_ref), (1 - core, away_ref))
    copies = [pltpu.make_async_copy(spec_ref.at[f], held, sems.at[i]) for i, (f, held) in enumerate(both)]
    for copy in copies:
        copy.start()
    ids = (row * n_col + col) * per + lax.broadcasted_iota(jnp.int32, (1, per), 1)
    rest = jnp.zeros((notes_ref.shape[1] - per, LANES), jnp.float32)
    wl_copy.wait()
    for at, ((f, held), copy) in enumerate(zip(both, copies)):
        copy.wait()
        squares = jnp.square(held[...].astype(jnp.float32))
        squares = squares[0] + squares[1]
        squares = sum(squares[:, at : at + LANES] for at in range(0, windows, LANES))
        columns = jnp.transpose(jnp.concatenate([squares, rest], axis=0))
        power = jnp.sum(columns, axis=0, keepdims=True)
        level = jnp.sum(jnp.where(ids == wl_held[f], power[:, :per], 0.0), axis=1, keepdims=True)
        notes_ref[2 * at : 2 * at + 1, :] = power
        notes_ref[2 * at + 1 : 2 * at + 2, :] = jnp.broadcast_to(level, power.shape)


def gate_kernel(n, *refs):
    out_ref, start = refs[-1], 0
    for ref in refs[:n]:
        out_ref[start : start + ref.shape[0], :] = ref[...]
        start += ref.shape[0]


def gated(values, others):
    rows, width = sum(v.shape[0] for v in values), values[0].shape[1]
    return kernel_call(
        functools.partial(gate_kernel, len(values)),
        [vmem((rows, width), values[0].dtype)],
        [*values, *others],
        [pltpu.VMEM] * (len(values) + len(others)),
        name="gate",
    )[0]


def send_kernel(token_ref, own_ref, other_ref, to_x_ref, to_y_ref):
    y = place()[4]
    half = to_y_ref.shape[-1]
    theirs = pl.ds(pl.multiple_of((1 - y) * half, half), half)
    for at, ref in enumerate((own_ref, other_ref)):
        to_x_ref[at] = ref[...]
        for part in range(ref.shape[0]):
            to_y_ref[at, part] = ref[part, :, theirs]


def steer_blocks(blocks, delays_ref, cos_ref, sin_ref, copy_ref=None):
    core = place()[2]
    rate = jnp.where(core == 0, cycle_rates[0], cycle_rates[1]).astype(jnp.float32)
    size = cos_ref.shape[0] // len(blocks)
    chunk = math.gcd(CHUNK, size)
    for index, (start, arrival) in enumerate(blocks):
        if arrival is not None:
            arrival.wait()

        @pl.loop(0, size // chunk)
        def _(i):
            here = pl.ds(pl.multiple_of(start + i * chunk, chunk), chunk)
            there = pl.ds(pl.multiple_of(index * size + i * chunk, chunk), chunk)
            delays = delays_ref[here, :]
            cos, sin = steer_rows(rate, delays)
            cos_ref[there, :] = cos
            sin_ref[there, :] = sin
            if copy_ref is not None:
                copy_ref[there, :] = delays.astype(copy_ref.dtype)


def steer_kernel(token_ref, delays_ref, cos_ref, sin_ref, out_ref):
    out_ref[...] = token_ref[...]
    steer_blocks([(0, None)], delays_ref, cos_ref, sin_ref)


def steer_far_kernel(starts, parts, token_ref, delays_ref, cos_ref, sin_ref, out_ref, *refs):
    *copy_ref, held_ref, sems = refs
    out_ref[...] = token_ref[...]
    firsts = starts()
    per = cos_ref.shape[0] // len(firsts)
    rows = per // parts
    blocks = []
    for j, first in enumerate(firsts):
        for part in range(parts):
            index = j * parts + part
            here = pl.ds(index * rows, rows)
            there = pl.ds(pl.multiple_of(first + part * rows, 8), rows)
            arrival = pltpu.make_async_copy(delays_ref.at[there, :], held_ref.at[here, :], sems.at[index])
            arrival.start()
            blocks.append((index * rows, arrival))
    steer_blocks(blocks, held_ref, cos_ref, sin_ref, *copy_ref)


def steering(token, delays):
    out = [vmem(delays.shape, jnp.bfloat16)] * 2 + [vmem(token.shape, token.dtype)]
    return kernel_call(steer_kernel, out, [token, delays], [pltpu.VMEM] * 2, name="steering")


def steering_far(starts, per, blocks, token, delays, copied=()):
    parts = math.gcd(per // CHUNK, 5)
    shape = (per * blocks, delays.shape[1])
    return kernel_call(
        functools.partial(steer_far_kernel, starts, parts),
        [vmem(shape, jnp.bfloat16)] * 2
        + [vmem(token.shape, token.dtype)]
        + [vmem(shape, t) for t in copied],
        [token, delays],
        [pltpu.VMEM, pltpu.HBM],
        scratch=[pltpu.VMEM(shape, delays.dtype), pltpu.SemaphoreType.DMA((blocks * parts,))],
        name="steering_far",
    )


def halves(total, block, bit, keep_ref, send_ref):
    for pair in range(keep_ref.shape[0] // block):
        out = pl.ds(pair * block, block)
        for ref, at in ((keep_ref, bit), (send_ref, 1 - bit)):
            rows = pl.ds(pl.multiple_of((2 * pair + at) * block, block), block)
            ref[out, :] = total[rows, :].astype(ref.dtype)


def beams_kernel(order, mine, block, kept, near_power_ref, far_ref, level_ref, own_ref, other_ref, from_ref, *refs):
    *steer, keep_ref, send_ref, token_ref, total_ref = refs
    token_ref[...] = level_ref[...]
    per = from_ref.shape[2]
    windows = mine(from_ref.shape[3])
    level = 0.5 * level_ref[...]
    real, imag = [], []
    for at in range(4):
        power = near_power_ref[at : at + 1] if at < 2 else far_ref[at - 2 : at - 1]
        gain = jnp.transpose(jnp.broadcast_to(lax.rsqrt(power + level), (8, level.shape[1])))[:per, :1]
        for part, parts in enumerate((real, imag)):
            near_ref = (own_ref, other_ref)[at % 2]
            spec = near_ref[part, :, windows] if at < 2 else from_ref[at - 2, part]
            parts.append(spec.astype(jnp.float32) * gain)
    total = None
    for group, members in enumerate(order):
        re, im = (jnp.concatenate([p[m] for m in members], axis=0).astype(jnp.bfloat16) for p in (real, imag))
        for left, right in (((re, im), steer[2 * group]), ((-im, re), steer[2 * group + 1])):
            term = lax.dot_general(
                right[...],
                jnp.concatenate(left, axis=1),
                (((0,), (0,)), ((), ())),
                preferred_element_type=jnp.float32,
            )
            total = term if total is None else total + term
    total_ref[...] = total
    halves(total_ref, block, kept(), keep_ref, send_ref)


def beams(order, mine, block, kept, near_power, far, level, own, other, arrived, steer, name):
    inputs = [near_power, far, level, own, other, arrived, *steer]
    rows, width = steer[0].shape[1], 2 * arrived.shape[-1]
    return kernel_call(
        functools.partial(beams_kernel, order, mine, block, kept),
        [
            vmem((rows // 2, width), jnp.float32),
            vmem((rows // 2, width), jnp.bfloat16),
            vmem(level.shape, level.dtype),
        ],
        inputs,
        [pltpu.VMEM] * len(inputs),
        scratch=[pltpu.VMEM((rows, width), jnp.float32)],
        limit=24,
        name=name,
    )


def step_kernel(block, axis, bit, given, keep_ref, other_ref, token_ref, *outs):
    if given:
        *outs, out_token_ref = outs if bit is None else (*outs[:2], outs[3], outs[2])
        out_token_ref[...] = token_ref[...]
    if bit is None:
        total = keep_ref[...] + other_ref[...].astype(jnp.float32)
        for ref in outs:
            ref[...] = total.astype(ref.dtype)
    else:
        keep_out, send_out, total_ref = outs
        total_ref[...] = keep_ref[...] + other_ref[...].astype(jnp.float32)
        index = lax.axis_index(axis)
        halves(total_ref, block, (index // bit) & 1, keep_out, send_out)


def exchange(keep, send, block, steps, given, name):
    token = yield
    for index, (axis, bit, _) in enumerate(steps):
        other = swap(send, axis, bit)
        rows, width = keep.shape
        scratch, cut = [], (None, None)
        if index + 1 == len(steps):
            out = [vmem((rows, width), jnp.bfloat16)]
        elif steps[index + 1][2]:
            out, cut = [vmem((rows // 2, width), t) for t in (jnp.float32, jnp.bfloat16)], steps[index + 1][:2]
            scratch = [pltpu.VMEM((rows, width), jnp.float32)]
        else:
            out = [vmem((rows, width), t) for t in (jnp.float32, jnp.bfloat16)]
        if index in given:
            out.append(vmem(token.shape, token.dtype))
        results = kernel_call(
            functools.partial(step_kernel, block, *cut, index in given),
            out,
            [keep, other, token],
            [pltpu.VMEM] * 3,
            scratch=scratch,
            name=name,
        )
        if index + 1 == len(steps):
            yield results[0]
        else:
            keep, send = results[:2]
            token = yield results[-1]


def field_kernel(scale, source_ref, near_r, far_r, keep_ref, send_ref):
    _, _, core, _, y = place()
    half = near_r.shape[1] // 2
    block = keep_ref.shape[2]

    def product(left, right):
        return lax.dot_general(left, right, (((1,), (1,)), ((), ())), preferred_element_type=jnp.float32)

    for ref, at in ((keep_ref, core), (send_ref, 1 - core)):
        rows = pl.ds(pl.multiple_of(at * block, block), block)
        real = imag = 0.0
        for bit, receiver in ((y, near_r), (1 - y, far_r)):
            s_re, s_im = (
                source_ref[:, pl.ds(pl.multiple_of((2 * part + bit) * half, half), half)] for part in (0, 1)
            )
            r_re, r_im = receiver[rows, :half], receiver[rows, half:]
            real += product(s_re, r_re) + product(s_im, r_im)
            imag += product(s_im, r_re) - product(s_re, r_im)
        ref[0] = real * scale
        ref[1] = imag * scale


def swap(value, axis, bit):
    size = lax.axis_size(axis)
    return lax.ppermute(value, axis, [(i, i ^ bit) for i in range(size)])


def choose(bit, first, second):
    return jnp.where(bit == 0, first, second)


def ordered(bit, own, other):
    return choose(bit, own, other), choose(bit, other, own)


def bits(size, start):
    found = []
    while start < size:
        found.append(start)
        start *= 2
    return found


def body(spectra, delays_s, delays_r, wl_index):
    n_row, n_col = lax.axis_size("row"), lax.axis_size("col")
    row, col, core, x, y = place()
    freqs, parts, per, windows = spectra.shape
    half = windows // 2
    padded = -(-per // LANES) * LANES

    spec_shape = vmem((parts, per, windows), spectra.dtype)
    notes, own, away = kernel_call(
        power_kernel,
        [vmem((4, padded), jnp.float32), spec_shape, spec_shape],
        [wl_index, spectra],
        [pltpu.HBM, pltpu.HBM],
        scratch=[pltpu.SMEM(wl_index.shape, wl_index.dtype), pltpu.SemaphoreType.DMA((3,))],
        name="power",
    )
    other = swap(away, "col", 1)

    def starts_r():
        return [(place()[0] ^ j) * per for j in (0, 1)]

    def starts_s(first, last):
        return lambda: [block_of(j, at) * per for j, at in ((0, 0), (0, 1), (1, 0), (1, 1))[first:last]]

    far = swap(notes, "col", 2)
    *steer_r, token, near_r = steering_far(starts_r, per, 2, notes[:1], delays_r, [jnp.int16])
    other_r = swap(near_r, "col", 1)
    across = swap(gated([notes[2:], far[2:]], [token]), "col", 1)
    power, far_x = jnp.concatenate([notes[:1], across[:1]]), jnp.concatenate([far[:1], across[2:3]])
    level = (notes[1:2] + far[1:2]) + (across[1:2] + across[3:])

    sent = [vmem((2, parts, per, w), spectra.dtype) for w in (windows, half)]
    to_x, to_y = kernel_call(send_kernel, sent, [level, own, other], [pltpu.VMEM] * 3, name="send")
    from_x, from_y = swap(to_x, "col", 2), swap(to_y, "row", 1)

    row_bits, col_bits = bits(n_row, 2), bits(n_col, 4)
    first, *others = [("row", bit) for bit in row_bits] + [("col", bit) for bit in col_bits]
    *steer_s, token = steering_far(starts_s(0, 2), per, 2, level, delays_s)
    level = level + swap(level, *first)
    cos, sin, next_token = steering_far(starts_s(2, 4), per, 2, level, delays_s)
    steer_s += [cos, sin]
    for step in others:
        level = gated([level], [token])
        level = level + swap(level, *step)
    cos, sin, token = steering(level, other_r)
    steer_r += [cos, sin]
    far_y = swap(gated([power, level], [from_y, next_token]), "row", 1)
    level = gated([level + far_y[2:]], [token])

    block_r, block_s = 2 * delays_r.shape[1] // n_col, delays_s.shape[1] // n_row
    keep_r, send_r, token = beams(
        ((0, 2), (1, 3)),
        lambda half: pl.ds(pl.multiple_of(y_of() * half, half), half),
        block_r,
        lambda: place()[3],
        power,
        far_y,
        level,
        own,
        other,
        from_y,
        steer_r,
        "beams_r",
    )
    keep_s, send_s, _ = beams(
        ((0, 1), (2, 3)), lambda windows: slice(None), block_s, y_of, power, far_x, token, own, other, from_x, steer_s, "beams_s"
    )
    r_steps = [("col", bit, True) for bit in [2, *col_bits]] + [("row", bit, False) for bit in row_bits]
    s_steps = [("row", bit, True) for bit in [1, *row_bits]] + [("col", bit, False) for bit in col_bits]
    late = 1
    r_chain = exchange(keep_r, send_r, block_r, r_steps, (), "step_r")
    s_chain = exchange(keep_s, send_s, block_s, s_steps, (late - 1,), "step_s")
    next(r_chain), next(s_chain)
    token = level
    for index in range(max(len(r_steps), len(s_steps))):
        if index < len(r_steps):
            receiver = r_chain.send(token if index == late else level)
        if index < len(s_steps):
            source = s_chain.send(level)
            if index == late - 1:
                token = source
    r_far = swap(receiver, "row", 1)

    block = delays_r.shape[1] // n_col
    shape = vmem((2, block_s, block), jnp.float32)
    scale = math.sqrt(windows) / (per * n_row * n_col)
    near, away = kernel_call(
        functools.partial(field_kernel, scale),
        [shape, shape],
        [source, receiver, r_far],
        [pltpu.VMEM] * 3,
        name="field",
    )
    far = swap(away, "col", 1)
    return jnp.stack(ordered(core, near, far)).swapaxes(2, 3)


def solution(mesh):
    in_specs = (P(None, None, ("row", "col"), None), P("row", None), P("col", None), P())
    out_specs = P(None, None, "col", "row")
    return jax.shard_map(body, mesh=mesh, in_specs=in_specs, out_specs=out_specs, check_vma=False)
```

```python
import functools
import math

import jax
import jax.numpy as jnp
from jax import lax
from jax.experimental import pallas as pl
from jax.experimental.pallas import tpu as pltpu
from jax.sharding import PartitionSpec as P

cycle_rates = (0.0361, 0.0596)
ROOT = math.sqrt(2.0)
SIN = (3.1415820121765137, -5.167142868041992, 2.5418989658355713, -0.5546361207962036)
COS = (0.9999999403953552, -4.934792995452881, 4.058412075042725, -1.3318800926208496, 0.2196967601776123)


def horner(z, terms):
    total = ROOT * terms[-1]
    for term in terms[-2::-1]:
        total = total * z + ROOT * term
    return total


def steer_rows(rate, delays):
    turns = rate * delays.astype(jnp.float32)
    turns = turns - jnp.round(turns)
    z = turns * turns
    half_sin = turns * horner(z, SIN)
    half_cos = horner(z, COS)
    return (1.0 - half_sin * half_sin).astype(jnp.bfloat16), (half_sin * half_cos).astype(jnp.bfloat16)


CHUNK = 32
LANES = 128


def place():
    row, col = lax.axis_index("row"), lax.axis_index("col")
    return row, col, col & 1, (col >> 1) & 1, row & 1


def y_of():
    return place()[4]


def block_of(j, at):
    _, col, core, x, _ = place()
    return (col >> 2) * 4 + (x ^ j) * 2 + (core ^ at)


def vmem(shape, dtype):
    return pltpu.VMEM(shape, dtype)


def kernel_call(body, out, inputs, spaces, scratch=(), limit=8, cost=1, name=None):
    held = [
        pltpu.with_memory_space_constraint(v, space) if space in (pltpu.HBM, pltpu.VMEM) else v
        for v, space in zip(inputs, spaces)
    ]
    return pl.pallas_call(
        body,
        out_shape=out,
        in_specs=[pl.BlockSpec(memory_space=space) for space in spaces],
        out_specs=[pl.BlockSpec(memory_space=pltpu.VMEM)] * len(out),
        scratch_shapes=list(scratch),
        compiler_params=pltpu.CompilerParams(vmem_limit_bytes=limit * 2**20),
        cost_estimate=pl.CostEstimate(flops=1, bytes_accessed=cost, transcendentals=0),
        name=name,
    )(*held)


def power_kernel(wl_ref, spec_ref, notes_ref, own_ref, away_ref, wl_held, sems):
    row, col, core, *_ = place()
    n_col = lax.axis_size("col")
    _, parts, per, windows = spec_ref.shape
    wl_copy = pltpu.make_async_copy(wl_ref, wl_held, sems.at[2])
    wl_copy.start()
    both = ((core, own_ref), (1 - core, away_ref))
    copies = [pltpu.make_async_copy(spec_ref.at[f], held, sems.at[i]) for i, (f, held) in enumerate(both)]
    for copy in copies:
        copy.start()
    ids = (row * n_col + col) * per + lax.broadcasted_iota(jnp.int32, (1, per), 1)
    rest = jnp.zeros((notes_ref.shape[1] - per, LANES), jnp.float32)
    wl_copy.wait()
    for at, ((f, held), copy) in enumerate(zip(both, copies)):
        copy.wait()
        squares = jnp.square(held[...].astype(jnp.float32))
        squares = squares[0] + squares[1]
        squares = sum(squares[:, at : at + LANES] for at in range(0, windows, LANES))
        columns = jnp.transpose(jnp.concatenate([squares, rest], axis=0))
        power = jnp.sum(columns, axis=0, keepdims=True)
        level = jnp.sum(jnp.where(ids == wl_held[f], power[:, :per], 0.0), axis=1, keepdims=True)
        notes_ref[2 * at : 2 * at + 1, :] = power
        notes_ref[2 * at + 1 : 2 * at + 2, :] = jnp.broadcast_to(level, power.shape)


def gate_kernel(n, *refs):
    out_ref, start = refs[-1], 0
    for ref in refs[:n]:
        out_ref[start : start + ref.shape[0], :] = ref[...]
        start += ref.shape[0]


def gated(values, others):
    rows, width = sum(v.shape[0] for v in values), values[0].shape[1]
    return kernel_call(
        functools.partial(gate_kernel, len(values)),
        [vmem((rows, width), values[0].dtype)],
        [*values, *others],
        [pltpu.VMEM] * (len(values) + len(others)),
        name="gate",
    )[0]


def send_kernel(token_ref, own_ref, other_ref, to_x_ref, to_y_ref):
    y = place()[4]
    half = to_y_ref.shape[-1]
    theirs = pl.ds(pl.multiple_of((1 - y) * half, half), half)
    for at, ref in enumerate((own_ref, other_ref)):
        to_x_ref[at] = ref[...]
        for part in range(ref.shape[0]):
            to_y_ref[at, part] = ref[part, :, theirs]


def by_parity(values, block):
    width = values.shape[1]
    if 2 * block != LANES or width % (2 * LANES):
        order = [at for parity in (0, 1) for at in range(parity * block, width, 2 * block)]
        return jnp.concatenate([values[:, at : at + block] for at in order], axis=1)
    low = lax.broadcasted_iota(jnp.int32, (values.shape[0], LANES), 1) < block
    even, odd = [], []
    for at in range(0, width, 2 * LANES):
        first, second = values[:, at : at + LANES], values[:, at + LANES : at + 2 * LANES]
        even.append(jnp.where(low, first, pltpu.roll(second, block, 1)))
        odd.append(jnp.where(low, pltpu.roll(first, block, 1), second))
    return jnp.concatenate(even + odd, axis=1)


def steer_blocks(blocks, delays_ref, cos_ref, sin_ref, copy_ref=None, block=None):
    core = place()[2]
    rate = jnp.where(core == 0, cycle_rates[0], cycle_rates[1]).astype(jnp.float32)
    size = cos_ref.shape[0] // len(blocks)
    chunk = math.gcd(CHUNK, size)
    for index, (start, arrival) in enumerate(blocks):
        if arrival is not None:
            arrival.wait()

        @pl.loop(0, size // chunk, unroll=math.gcd(size // chunk, 10) if block else 1)
        def _(i):
            here = pl.ds(pl.multiple_of(start + i * chunk, chunk), chunk)
            there = pl.ds(pl.multiple_of(index * size + i * chunk, chunk), chunk)
            delays = delays_ref[here, :]
            if block:
                delays = by_parity(delays, block)
            cos, sin = steer_rows(rate, delays)
            cos_ref[there, :] = cos
            sin_ref[there, :] = sin
            if copy_ref is not None:
                copy_ref[there, :] = delays.astype(copy_ref.dtype)


def steer_kernel(token_ref, delays_ref, cos_ref, sin_ref, out_ref):
    out_ref[...] = token_ref[...]
    steer_blocks([(0, None)], delays_ref, cos_ref, sin_ref)


def steer_far_kernel(starts, parts, block, token_ref, delays_ref, cos_ref, sin_ref, out_ref, *refs):
    *copy_ref, held_ref, sems = refs
    out_ref[...] = token_ref[...]
    firsts = starts()
    per = cos_ref.shape[0] // len(firsts)
    rows = per // parts
    blocks = []
    for j, first in enumerate(firsts):
        for part in range(parts):
            index = j * parts + part
            here = pl.ds(index * rows, rows)
            there = pl.ds(pl.multiple_of(first + part * rows, 8), rows)
            arrival = pltpu.make_async_copy(delays_ref.at[there, :], held_ref.at[here, :], sems.at[index])
            arrival.start()
            blocks.append((index * rows, arrival))
    steer_blocks(blocks, held_ref, cos_ref, sin_ref, *(copy_ref or [None]), block)


def steering(token, delays):
    out = [vmem(delays.shape, jnp.bfloat16)] * 2 + [vmem(token.shape, token.dtype)]
    return kernel_call(steer_kernel, out, [token, delays], [pltpu.VMEM] * 2, name="steering")


def steering_far(starts, per, blocks, token, delays, copied=(), block=None):
    parts = math.gcd(per // CHUNK, 1 if block else 5)
    shape = (per * blocks, delays.shape[1])
    return kernel_call(
        functools.partial(steer_far_kernel, starts, parts, block),
        [vmem(shape, jnp.bfloat16)] * 2
        + [vmem(token.shape, token.dtype)]
        + [vmem(shape, t) for t in copied],
        [token, delays],
        [pltpu.VMEM, pltpu.HBM],
        scratch=[pltpu.VMEM(shape, delays.dtype), pltpu.SemaphoreType.DMA((blocks * parts,))],
        name="steering_far",
    )


def halves(total, block, bit, keep_ref, send_ref):
    for pair in range(keep_ref.shape[0] // block):
        out = pl.ds(pair * block, block)
        for ref, at in ((keep_ref, bit), (send_ref, 1 - bit)):
            rows = pl.ds(pl.multiple_of((2 * pair + at) * block, block), block)
            ref[out, :] = total[rows, :].astype(ref.dtype)


def beams_kernel(order, mine, block, kept, only, near_power_ref, far_ref, level_ref, own_ref, other_ref, from_ref, *refs):
    if only is None:
        *steer, keep_ref, send_ref, total_ref = refs
        beams_of = slice(None)
    else:
        *steer, total_ref = refs
        beams_of = pl.ds(pl.multiple_of(only() * total_ref.shape[0], total_ref.shape[0]), total_ref.shape[0])
    per = from_ref.shape[2]
    windows = mine(from_ref.shape[3])
    width = total_ref.shape[1] // 2
    powers = jnp.concatenate([near_power_ref[...], far_ref[:2]], axis=0)
    gains = lax.rsqrt(powers + 0.5 * level_ref[...])
    gains = jnp.transpose(jnp.concatenate([gains, gains], axis=0))[:per]
    scaled = []
    for at in range(4):
        near_ref = (own_ref, other_ref)[at % 2]
        spec = [near_ref[part, :, windows] if at < 2 else from_ref[at - 2, part] for part in (0, 1)]
        scaled.append(jnp.concatenate(spec, axis=1).astype(jnp.float32) * gains[:, at : at + 1])
    sums = [0.0, 0.0]
    for group, members in enumerate(order):
        right = jnp.concatenate([scaled[m] for m in members], axis=0).astype(jnp.bfloat16)
        for at in (0, 1):
            sums[at] += lax.dot_general(
                steer[2 * group + at][:, beams_of], right, (((0,), (0,)), ((), ())), preferred_element_type=jnp.float32
            )
    with_cos, with_sin = sums
    total_ref[:, :width] = (with_cos[:, :width] - with_sin[:, width:]).astype(total_ref.dtype)
    total_ref[:, width:] = (with_cos[:, width:] + with_sin[:, :width]).astype(total_ref.dtype)
    if only is None:
        halves(total_ref, block, kept(), keep_ref, send_ref)


def beams(order, mine, block, kept, near_power, far, level, own, other, arrived, steer, name, only=None, dtype=None):
    inputs = [near_power, far, level, own, other, arrived, *steer]
    rows, width = steer[0].shape[1], 2 * arrived.shape[-1]
    out = [vmem((rows // 2, width), t) for t in ((jnp.float32, jnp.bfloat16) if only is None else (dtype,))]
    return kernel_call(
        functools.partial(beams_kernel, order, mine, block, kept, only),
        out,
        inputs,
        [pltpu.VMEM] * len(inputs),
        scratch=[pltpu.VMEM((rows, width), jnp.float32)] if only is None else [],
        limit=24,
        name=name,
    )


def step_kernel(block, axis, bit, given, keep_ref, other_ref, token_ref, *outs):
    if given:
        *outs, out_token_ref = outs if bit is None else (*outs[:2], outs[3], outs[2])
        out_token_ref[...] = token_ref[...]
    if bit is None:
        total = keep_ref[...] + other_ref[...].astype(jnp.float32)
        for ref in outs:
            ref[...] = total.astype(ref.dtype)
    else:
        keep_out, send_out, total_ref = outs
        total_ref[...] = keep_ref[...] + other_ref[...].astype(jnp.float32)
        index = lax.axis_index(axis)
        halves(total_ref, block, (index // bit) & 1, keep_out, send_out)


def exchange(keep, send, block, steps, given, name):
    token = yield
    for index, (axis, bit, _) in enumerate(steps):
        other = swap(send, axis, bit)
        rows, width = keep.shape
        scratch, cut = [], (None, None)
        if index + 1 == len(steps):
            out = [vmem((rows, width), jnp.bfloat16)]
        elif steps[index + 1][2]:
            out, cut = [vmem((rows // 2, width), t) for t in (jnp.float32, jnp.bfloat16)], steps[index + 1][:2]
            scratch = [pltpu.VMEM((rows, width), jnp.float32)]
        else:
            out = [vmem((rows, width), t) for t in (jnp.float32, jnp.bfloat16)]
        if index in given:
            out.append(vmem(token.shape, token.dtype))
        results = kernel_call(
            functools.partial(step_kernel, block, *cut, index in given),
            out,
            [keep, other, token],
            [pltpu.VMEM] * 3,
            scratch=scratch,
            name=name,
        )
        if index + 1 == len(steps):
            yield results[0]
        else:
            keep, send = results[:2]
            token = yield results[-1]


def field_kernel(scale, source_ref, near_r, far_r, keep_ref, send_ref):
    _, _, core, _, y = place()
    half = near_r.shape[1] // 2
    block = keep_ref.shape[2]

    def product(left, right):
        return lax.dot_general(left, right, (((1,), (1,)), ((), ())), preferred_element_type=jnp.float32)

    for ref, at in ((keep_ref, core), (send_ref, 1 - core)):
        rows = pl.ds(pl.multiple_of(at * block, block), block)
        real = imag = 0.0
        for bit, receiver in ((y, near_r), (1 - y, far_r)):
            s_re, s_im = (
                source_ref[:, pl.ds(pl.multiple_of((2 * part + bit) * half, half), half)] for part in (0, 1)
            )
            r_re, r_im = receiver[rows, :half], receiver[rows, half:]
            real += product(s_re, r_re) + product(s_im, r_im)
            imag += product(s_im, r_re) - product(s_re, r_im)
        ref[0] = real * scale
        ref[1] = imag * scale


def swap(value, axis, bit):
    size = lax.axis_size(axis)
    return lax.ppermute(value, axis, [(i, i ^ bit) for i in range(size)])


def choose(bit, first, second):
    return jnp.where(bit == 0, first, second)


def ordered(bit, own, other):
    return choose(bit, own, other), choose(bit, other, own)


def bits(size, start):
    found = []
    while start < size:
        found.append(start)
        start *= 2
    return found


def body(spectra, delays_s, delays_r, wl_index):
    n_row, n_col = lax.axis_size("row"), lax.axis_size("col")
    row, col, core, x, y = place()
    freqs, parts, per, windows = spectra.shape
    half = windows // 2
    padded = -(-per // LANES) * LANES

    spec_shape = vmem((parts, per, windows), spectra.dtype)
    block_r, block_s = 2 * delays_r.shape[1] // n_col, delays_s.shape[1] // n_row
    notes, own, away = kernel_call(
        power_kernel,
        [vmem((4, padded), jnp.float32), spec_shape, spec_shape],
        [wl_index, spectra],
        [pltpu.HBM, pltpu.HBM],
        scratch=[pltpu.SMEM(wl_index.shape, wl_index.dtype), pltpu.SemaphoreType.DMA((3,))],
        name="power",
    )
    other = swap(away, "col", 1)

    def starts_r():
        return [(place()[0] ^ j) * per for j in (0, 1)]

    def starts_s(first, last):
        return lambda: [block_of(j, at) * per for j, at in ((0, 0), (0, 1), (1, 0), (1, 1))[first:last]]

    far = swap(notes, "col", 2)
    *steer_r, token, near_r = steering_far(starts_r, per, 2, notes[:1], delays_r, [jnp.int16])
    other_r = swap(near_r, "col", 1)
    across = swap(gated([notes[2:], far[2:]], [token]), "col", 1)
    power, far_x = jnp.concatenate([notes[:1], across[:1]]), jnp.concatenate([far[:1], across[2:3]])
    level = (notes[1:2] + far[1:2]) + (across[1:2] + across[3:])

    sent = [vmem((2, parts, per, w), spectra.dtype) for w in (windows, half)]
    to_x, to_y = kernel_call(send_kernel, sent, [level, own, other], [pltpu.VMEM] * 3, name="send")
    from_x, from_y = swap(to_x, "col", 2), swap(to_y, "row", 1)

    row_bits, col_bits = bits(n_row, 2), bits(n_col, 4)
    first, *others = [("row", bit) for bit in row_bits] + [("col", bit) for bit in col_bits]
    *steer_s, token = steering_far(starts_s(0, 2), per, 2, level, delays_s, block=block_s)
    level = level + swap(level, *first)
    cos, sin, next_token = steering_far(starts_s(2, 4), per, 2, level, delays_s, block=block_s)
    steer_s += [cos, sin]
    for step in others:
        level = gated([level], [token])
        level = level + swap(level, *step)
    cos, sin, token = steering(level, other_r)
    steer_r += [cos, sin]
    far_y = swap(gated([power, level], [from_y, next_token]), "row", 1)
    level = gated([level + far_y[2:]], [token])

    keep_r, send_r = beams(
        ((0, 2), (1, 3)),
        lambda half: pl.ds(pl.multiple_of(y_of() * half, half), half),
        block_r,
        lambda: place()[3],
        power,
        far_y,
        level,
        own,
        other,
        from_y,
        steer_r,
        "beams_r",
    )
    (send_s,), (keep_s,) = (
        beams(
            ((0, 1), (2, 3)),
            lambda windows: slice(None),
            None,
            None,
            power,
            far_x,
            level,
            own,
            other,
            from_x,
            steer_s,
            "beams_s",
            only,
            dtype,
        )
        for only, dtype in ((lambda: 1 - y_of(), jnp.bfloat16), (y_of, jnp.float32))
    )
    r_steps = [("col", bit, True) for bit in [2, *col_bits]] + [("row", bit, False) for bit in row_bits]
    s_steps = [("row", bit, True) for bit in [1, *row_bits]] + [("col", bit, False) for bit in col_bits]
    late = 1
    r_chain = exchange(keep_r, send_r, block_r, r_steps, (), "step_r")
    s_chain = exchange(keep_s, send_s, block_s, s_steps, (late - 1,), "step_s")
    next(r_chain), next(s_chain)
    token = level
    for index in range(max(len(r_steps), len(s_steps))):
        if index < len(r_steps):
            receiver = r_chain.send(token if index == late else level)
        if index < len(s_steps):
            source = s_chain.send(level)
            if index == late - 1:
                token = source
    r_far = swap(receiver, "row", 1)

    block = delays_r.shape[1] // n_col
    shape = vmem((2, block_s, block), jnp.float32)
    scale = math.sqrt(windows) / (per * n_row * n_col)
    near, away = kernel_call(
        functools.partial(field_kernel, scale),
        [shape, shape],
        [source, receiver, r_far],
        [pltpu.VMEM] * 3,
        name="field",
    )
    far = swap(away, "col", 1)
    return jnp.stack(ordered(core, near, far)).swapaxes(2, 3)


def solution(mesh):
    in_specs = (P(None, None, ("row", "col"), None), P("row", None), P("col", None), P())
    out_specs = P(None, None, "col", "row")
    return jax.shard_map(body, mesh=mesh, in_specs=in_specs, out_specs=out_specs, check_vma=False)
```

```python
import functools
import math

import jax
import jax.numpy as jnp
from jax import lax
from jax.experimental import pallas as pl
from jax.experimental.pallas import tpu as pltpu
from jax.sharding import PartitionSpec as P

cycle_rates = (0.0361, 0.0596)
ROOT = math.sqrt(2.0)
SIN = (3.1415820121765137, -5.167142868041992, 2.5418989658355713, -0.5546361207962036)
COS = (0.9999999403953552, -4.934792995452881, 4.058412075042725, -1.3318800926208496, 0.2196967601776123)


def horner(z, terms):
    total = ROOT * terms[-1]
    for term in terms[-2::-1]:
        total = total * z + ROOT * term
    return total


def steer_rows(rate, delays):
    turns = rate * delays.astype(jnp.float32)
    turns = turns - jnp.round(turns)
    z = turns * turns
    half_sin = turns * horner(z, SIN)
    half_cos = horner(z, COS)
    return (1.0 - half_sin * half_sin).astype(jnp.bfloat16), (half_sin * half_cos).astype(jnp.bfloat16)


CHUNK = 32
LANES = 128


def place():
    row, col = lax.axis_index("row"), lax.axis_index("col")
    return row, col, col & 1, (col >> 1) & 1, row & 1


def y_of():
    return place()[4]


def block_of(j, at):
    _, col, core, x, _ = place()
    return (col >> 2) * 4 + (x ^ j) * 2 + (core ^ at)


def vmem(shape, dtype):
    return pltpu.VMEM(shape, dtype)


def kernel_call(body, out, inputs, spaces, scratch=(), limit=8, cost=1, name=None):
    held = [
        pltpu.with_memory_space_constraint(v, space) if space in (pltpu.HBM, pltpu.VMEM) else v
        for v, space in zip(inputs, spaces)
    ]
    return pl.pallas_call(
        body,
        out_shape=out,
        in_specs=[pl.BlockSpec(memory_space=space) for space in spaces],
        out_specs=[pl.BlockSpec(memory_space=pltpu.VMEM)] * len(out),
        scratch_shapes=list(scratch),
        compiler_params=pltpu.CompilerParams(vmem_limit_bytes=limit * 2**20),
        cost_estimate=pl.CostEstimate(flops=1, bytes_accessed=cost, transcendentals=0),
        name=name,
    )(*held)


def power_kernel(wl_ref, spec_ref, notes_ref, own_ref, away_ref, wl_held, sems):
    row, col, core, *_ = place()
    n_col = lax.axis_size("col")
    _, parts, per, windows = spec_ref.shape
    wl_copy = pltpu.make_async_copy(wl_ref, wl_held, sems.at[2])
    wl_copy.start()
    both = ((core, own_ref), (1 - core, away_ref))
    copies = [pltpu.make_async_copy(spec_ref.at[f], held, sems.at[i]) for i, (f, held) in enumerate(both)]
    for copy in copies:
        copy.start()
    ids = (row * n_col + col) * per + lax.broadcasted_iota(jnp.int32, (1, per), 1)
    rest = jnp.zeros((notes_ref.shape[1] - per, LANES), jnp.float32)
    wl_copy.wait()
    for at, ((f, held), copy) in enumerate(zip(both, copies)):
        copy.wait()
        squares = jnp.square(held[...].astype(jnp.float32))
        squares = squares[0] + squares[1]
        squares = sum(squares[:, at : at + LANES] for at in range(0, windows, LANES))
        columns = jnp.transpose(jnp.concatenate([squares, rest], axis=0))
        power = jnp.sum(columns, axis=0, keepdims=True)
        level = jnp.sum(jnp.where(ids == wl_held[f], power[:, :per], 0.0), axis=1, keepdims=True)
        notes_ref[2 * at : 2 * at + 1, :] = power
        notes_ref[2 * at + 1 : 2 * at + 2, :] = jnp.broadcast_to(level, power.shape)


def gate_kernel(n, *refs):
    out_ref, start = refs[-1], 0
    for ref in refs[:n]:
        out_ref[start : start + ref.shape[0], :] = ref[...]
        start += ref.shape[0]


def gated(values, others):
    rows, width = sum(v.shape[0] for v in values), values[0].shape[1]
    return kernel_call(
        functools.partial(gate_kernel, len(values)),
        [vmem((rows, width), values[0].dtype)],
        [*values, *others],
        [pltpu.VMEM] * (len(values) + len(others)),
        name="gate",
    )[0]


def send_kernel(token_ref, own_ref, other_ref, to_x_ref, to_y_ref):
    y = place()[4]
    half = to_y_ref.shape[-1]
    theirs = pl.ds(pl.multiple_of((1 - y) * half, half), half)
    for at, ref in enumerate((own_ref, other_ref)):
        to_x_ref[at] = ref[...]
        for part in range(ref.shape[0]):
            to_y_ref[at, part] = ref[part, :, theirs]


def by_parity(values, block):
    width = values.shape[1]
    if 2 * block != LANES or width % (2 * LANES):
        order = [at for parity in (0, 1) for at in range(parity * block, width, 2 * block)]
        return jnp.concatenate([values[:, at : at + block] for at in order], axis=1)
    low = lax.broadcasted_iota(jnp.int32, (values.shape[0], LANES), 1) < block
    even, odd = [], []
    for at in range(0, width, 2 * LANES):
        first, second = values[:, at : at + LANES], values[:, at + LANES : at + 2 * LANES]
        even.append(jnp.where(low, first, pltpu.roll(second, block, 1)))
        odd.append(jnp.where(low, pltpu.roll(first, block, 1), second))
    return jnp.concatenate(even + odd, axis=1)


def steer_blocks(blocks, delays_ref, cos_ref, sin_ref, copy_ref=None, block=None):
    core = place()[2]
    rate = jnp.where(core == 0, cycle_rates[0], cycle_rates[1]).astype(jnp.float32)
    size = cos_ref.shape[0] // len(blocks)
    chunk = math.gcd(CHUNK, size)
    for index, (start, arrival) in enumerate(blocks):
        if arrival is not None:
            arrival.wait()

        @pl.loop(0, size // chunk, unroll=math.gcd(size // chunk, 10))
        def _(i):
            here = pl.ds(pl.multiple_of(start + i * chunk, chunk), chunk)
            there = pl.ds(pl.multiple_of(index * size + i * chunk, chunk), chunk)
            delays = delays_ref[here, :]
            if block:
                delays = by_parity(delays, block)
            cos, sin = steer_rows(rate, delays)
            cos_ref[there, :] = cos
            sin_ref[there, :] = sin
            if copy_ref is not None:
                copy_ref[there, :] = delays.astype(copy_ref.dtype)


def steer_kernel(token_ref, delays_ref, cos_ref, sin_ref, out_ref):
    out_ref[...] = token_ref[...]
    steer_blocks([(0, None)], delays_ref, cos_ref, sin_ref)


def steer_far_kernel(starts, parts, block, token_ref, delays_ref, cos_ref, sin_ref, out_ref, *refs):
    *copy_ref, held_ref, sems = refs
    out_ref[...] = token_ref[...]
    firsts = starts()
    per = cos_ref.shape[0] // len(firsts)
    rows = per // parts
    blocks = []
    for j, first in enumerate(firsts):
        for part in range(parts):
            index = j * parts + part
            here = pl.ds(index * rows, rows)
            there = pl.ds(pl.multiple_of(first + part * rows, 8), rows)
            arrival = pltpu.make_async_copy(delays_ref.at[there, :], held_ref.at[here, :], sems.at[index])
            arrival.start()
            blocks.append((index * rows, arrival))
    steer_blocks(blocks, held_ref, cos_ref, sin_ref, *(copy_ref or [None]), block)


def steering(token, delays):
    out = [vmem(delays.shape, jnp.bfloat16)] * 2 + [vmem(token.shape, token.dtype)]
    return kernel_call(steer_kernel, out, [token, delays], [pltpu.VMEM] * 2, name="steering")


def steering_far(starts, per, blocks, token, delays, copied=(), block=None):
    parts = math.gcd(per // CHUNK, 1 if block else 2)
    shape = (per * blocks, delays.shape[1])
    return kernel_call(
        functools.partial(steer_far_kernel, starts, parts, block),
        [vmem(shape, jnp.bfloat16)] * 2
        + [vmem(token.shape, token.dtype)]
        + [vmem(shape, t) for t in copied],
        [token, delays],
        [pltpu.VMEM, pltpu.HBM],
        scratch=[pltpu.VMEM(shape, delays.dtype), pltpu.SemaphoreType.DMA((blocks * parts,))],
        name="steering_far",
    )


def halves(total, block, bit, keep_ref, send_ref):
    for pair in range(keep_ref.shape[0] // block):
        out = pl.ds(pair * block, block)
        for ref, at in ((keep_ref, bit), (send_ref, 1 - bit)):
            rows = pl.ds(pl.multiple_of((2 * pair + at) * block, block), block)
            ref[out, :] = total[rows, :].astype(ref.dtype)


def beams_kernel(order, mine, block, kept, only, near_power_ref, far_ref, level_ref, own_ref, other_ref, from_ref, *refs):
    if only is None:
        *steer, keep_ref, send_ref, total_ref = refs
        beams_of = slice(None)
    else:
        *steer, total_ref = refs
        beams_of = pl.ds(pl.multiple_of(only() * total_ref.shape[0], total_ref.shape[0]), total_ref.shape[0])
    per = from_ref.shape[2]
    windows = mine(from_ref.shape[3])
    width = total_ref.shape[1] // 2
    powers = jnp.concatenate([near_power_ref[...], far_ref[:2]], axis=0)
    gains = lax.rsqrt(powers + 0.5 * level_ref[...])
    gains = jnp.transpose(jnp.concatenate([gains, gains], axis=0))[:per]
    scaled = []
    for at in range(4):
        near_ref = (own_ref, other_ref)[at % 2]
        spec = [near_ref[part, :, windows] if at < 2 else from_ref[at - 2, part] for part in (0, 1)]
        scaled.append(jnp.concatenate(spec, axis=1).astype(jnp.float32) * gains[:, at : at + 1])
    sums = [0.0, 0.0]
    for group, members in enumerate(order):
        right = jnp.concatenate([scaled[m] for m in members], axis=0).astype(jnp.bfloat16)
        for at in (0, 1):
            sums[at] += lax.dot_general(
                steer[2 * group + at][:, beams_of], right, (((0,), (0,)), ((), ())), preferred_element_type=jnp.float32
            )
    with_cos, with_sin = sums
    total_ref[:, :width] = (with_cos[:, :width] - with_sin[:, width:]).astype(total_ref.dtype)
    total_ref[:, width:] = (with_cos[:, width:] + with_sin[:, :width]).astype(total_ref.dtype)
    if only is None:
        halves(total_ref, block, kept(), keep_ref, send_ref)


def beams(order, mine, block, kept, near_power, far, level, own, other, arrived, steer, name, only=None, dtype=None):
    inputs = [near_power, far, level, own, other, arrived, *steer]
    rows, width = steer[0].shape[1], 2 * arrived.shape[-1]
    out = [vmem((rows // 2, width), t) for t in ((jnp.float32, jnp.bfloat16) if only is None else (dtype,))]
    return kernel_call(
        functools.partial(beams_kernel, order, mine, block, kept, only),
        out,
        inputs,
        [pltpu.VMEM] * len(inputs),
        scratch=[pltpu.VMEM((rows, width), jnp.float32)] if only is None else [],
        limit=24,
        name=name,
    )


def step_kernel(block, axis, bit, given, keep_ref, other_ref, token_ref, *outs):
    if given:
        *outs, out_token_ref = outs if bit is None else (*outs[:2], outs[3], outs[2])
        out_token_ref[...] = token_ref[...]
    if bit is None:
        total = keep_ref[...] + other_ref[...].astype(jnp.float32)
        for ref in outs:
            ref[...] = total.astype(ref.dtype)
    else:
        keep_out, send_out, total_ref = outs
        total_ref[...] = keep_ref[...] + other_ref[...].astype(jnp.float32)
        index = lax.axis_index(axis)
        halves(total_ref, block, (index // bit) & 1, keep_out, send_out)


def exchange(keep, send, block, steps, given, name):
    token = yield
    for index, (axis, bit, _) in enumerate(steps):
        other = swap(send, axis, bit)
        rows, width = keep.shape
        scratch, cut = [], (None, None)
        if index + 1 == len(steps):
            out = [vmem((rows, width), jnp.bfloat16)]
        elif steps[index + 1][2]:
            out, cut = [vmem((rows // 2, width), t) for t in (jnp.float32, jnp.bfloat16)], steps[index + 1][:2]
            scratch = [pltpu.VMEM((rows, width), jnp.float32)]
        else:
            out = [vmem((rows, width), t) for t in (jnp.float32, jnp.bfloat16)]
        if index in given:
            out.append(vmem(token.shape, token.dtype))
        results = kernel_call(
            functools.partial(step_kernel, block, *cut, index in given),
            out,
            [keep, other, token],
            [pltpu.VMEM] * 3,
            scratch=scratch,
            name=name,
        )
        if index + 1 == len(steps):
            yield results[0]
        else:
            keep, send = results[:2]
            token = yield results[-1]


def field_kernel(scale, mine, source_ref, near_r, far_r, field_ref):
    _, _, core, _, y = place()
    half = near_r.shape[1] // 2
    block = field_ref.shape[2]

    def product(left, right):
        return lax.dot_general(left, right, (((1,), (1,)), ((), ())), preferred_element_type=jnp.float32)

    rows = pl.ds(pl.multiple_of((core if mine else 1 - core) * block, block), block)
    real = imag = 0.0
    for bit, receiver in ((y, near_r), (1 - y, far_r)):
        s_re, s_im = (
            source_ref[:, pl.ds(pl.multiple_of((2 * part + bit) * half, half), half)] for part in (0, 1)
        )
        r_re, r_im = receiver[rows, :half], receiver[rows, half:]
        real += product(s_re, r_re) + product(s_im, r_im)
        imag += product(s_im, r_re) - product(s_re, r_im)
    field_ref[0] = real * scale
    field_ref[1] = imag * scale


def swap(value, axis, bit):
    size = lax.axis_size(axis)
    return lax.ppermute(value, axis, [(i, i ^ bit) for i in range(size)])


def choose(bit, first, second):
    return jnp.where(bit == 0, first, second)


def ordered(bit, own, other):
    return choose(bit, own, other), choose(bit, other, own)


def bits(size, start):
    found = []
    while start < size:
        found.append(start)
        start *= 2
    return found


def body(spectra, delays_s, delays_r, wl_index):
    n_row, n_col = lax.axis_size("row"), lax.axis_size("col")
    row, col, core, x, y = place()
    freqs, parts, per, windows = spectra.shape
    half = windows // 2
    padded = -(-per // LANES) * LANES

    spec_shape = vmem((parts, per, windows), spectra.dtype)
    block_r, block_s = 2 * delays_r.shape[1] // n_col, delays_s.shape[1] // n_row
    notes, own, away = kernel_call(
        power_kernel,
        [vmem((4, padded), jnp.float32), spec_shape, spec_shape],
        [wl_index, spectra],
        [pltpu.HBM, pltpu.HBM],
        scratch=[pltpu.SMEM(wl_index.shape, wl_index.dtype), pltpu.SemaphoreType.DMA((3,))],
        name="power",
    )
    other = swap(away, "col", 1)

    def starts_r():
        return [(place()[0] ^ j) * per for j in (0, 1)]

    def starts_s(first, last):
        return lambda: [block_of(j, at) * per for j, at in ((0, 0), (0, 1), (1, 0), (1, 1))[first:last]]

    far = swap(notes, "col", 2)
    *steer_r, token, near_r = steering_far(starts_r, per, 2, notes[:1], delays_r, [jnp.int16])
    other_r = swap(near_r, "col", 1)
    across = swap(gated([notes[2:], far[2:]], [token]), "col", 1)
    power, far_x = jnp.concatenate([notes[:1], across[:1]]), jnp.concatenate([far[:1], across[2:3]])
    level = (notes[1:2] + far[1:2]) + (across[1:2] + across[3:])

    sent = [vmem((2, parts, per, w), spectra.dtype) for w in (windows, half)]
    to_x, to_y = kernel_call(send_kernel, sent, [level, own, other], [pltpu.VMEM] * 3, name="send")
    from_x, from_y = swap(to_x, "col", 2), swap(to_y, "row", 1)

    row_bits, col_bits = bits(n_row, 2), bits(n_col, 4)
    first, *others = [("row", bit) for bit in row_bits] + [("col", bit) for bit in col_bits]
    *steer_s, token = steering_far(starts_s(0, 2), per, 2, level, delays_s, block=block_s)
    level = level + swap(level, *first)
    cos, sin, next_token = steering_far(starts_s(2, 4), per, 2, level, delays_s, block=block_s)
    steer_s += [cos, sin]
    for step in others:
        level = gated([level], [token])
        level = level + swap(level, *step)
    cos, sin, token = steering(level, other_r)
    steer_r += [cos, sin]
    far_y = swap(gated([power, level], [from_y, next_token]), "row", 1)
    level = gated([level + far_y[2:]], [token])

    keep_r, send_r = beams(
        ((0, 2), (1, 3)),
        lambda half: pl.ds(pl.multiple_of(y_of() * half, half), half),
        block_r,
        lambda: place()[3],
        power,
        far_y,
        level,
        own,
        other,
        from_y,
        steer_r,
        "beams_r",
    )
    (send_s,), (keep_s,) = (
        beams(
            ((0, 1), (2, 3)),
            lambda windows: slice(None),
            None,
            None,
            power,
            far_x,
            level,
            own,
            other,
            from_x,
            steer_s,
            "beams_s",
            only,
            dtype,
        )
        for only, dtype in ((lambda: 1 - y_of(), jnp.bfloat16), (y_of, jnp.float32))
    )
    r_steps = [("col", bit, True) for bit in [2, *col_bits]] + [("row", bit, False) for bit in row_bits]
    s_steps = [("row", bit, True) for bit in [1, *row_bits]] + [("col", bit, False) for bit in col_bits]
    late = 1
    r_chain = exchange(keep_r, send_r, block_r, r_steps, (), "step_r")
    s_chain = exchange(keep_s, send_s, block_s, s_steps, (late - 1,), "step_s")
    next(r_chain), next(s_chain)
    token = level
    for index in range(max(len(r_steps), len(s_steps))):
        if index < len(r_steps):
            receiver = r_chain.send(token if index == late else level)
        if index < len(s_steps):
            source = s_chain.send(level)
            if index == late - 1:
                token = source
    r_far = swap(receiver, "row", 1)

    block = delays_r.shape[1] // n_col
    shape = vmem((2, block_s, block), jnp.float32)
    scale = math.sqrt(windows) / (per * n_row * n_col)
    away, near = (
        kernel_call(
            functools.partial(field_kernel, scale, mine),
            [shape],
            [source, receiver, r_far],
            [pltpu.VMEM] * 3,
            name="field",
        )[0]
        for mine in (False, True)
    )
    far = swap(away, "col", 1)
    return jnp.stack(ordered(core, near, far)).swapaxes(2, 3)


def solution(mesh):
    in_specs = (P(None, None, ("row", "col"), None), P("row", None), P("col", None), P())
    out_specs = P(None, None, "col", "row")
    return jax.shard_map(body, mesh=mesh, in_specs=in_specs, out_specs=out_specs, check_vma=False)
```

```python
import functools
import math

import jax
import jax.numpy as jnp
from jax import lax
from jax.experimental import pallas as pl
from jax.experimental.pallas import tpu as pltpu
from jax.sharding import PartitionSpec as P

cycle_rates = (0.0361, 0.0596)
ROOT = math.sqrt(2.0)
SIN = (3.1415820121765137, -5.167142868041992, 2.5418989658355713, -0.5546361207962036)
COS = (0.9999999403953552, -4.934792995452881, 4.058412075042725, -1.3318800926208496, 0.2196967601776123)


def horner(z, terms):
    total = ROOT * terms[-1]
    for term in terms[-2::-1]:
        total = total * z + ROOT * term
    return total


def steer_rows(rate, delays):
    turns = rate * delays.astype(jnp.float32)
    turns = turns - jnp.round(turns)
    z = turns * turns
    half_sin = turns * horner(z, SIN)
    half_cos = horner(z, COS)
    return (1.0 - half_sin * half_sin).astype(jnp.bfloat16), (half_sin * half_cos).astype(jnp.bfloat16)


CHUNK = 32
LANES = 128


def place():
    row, col = lax.axis_index("row"), lax.axis_index("col")
    return row, col, col & 1, (col >> 1) & 1, row & 1


def y_of():
    return place()[4]


def block_of(j, at):
    _, col, core, x, _ = place()
    return (col >> 2) * 4 + (x ^ j) * 2 + (core ^ at)


def vmem(shape, dtype):
    return pltpu.VMEM(shape, dtype)


def kernel_call(body, out, inputs, spaces, scratch=(), limit=8, cost=1, name=None):
    held = [
        pltpu.with_memory_space_constraint(v, space) if space in (pltpu.HBM, pltpu.VMEM) else v
        for v, space in zip(inputs, spaces)
    ]
    return pl.pallas_call(
        body,
        out_shape=out,
        in_specs=[pl.BlockSpec(memory_space=space) for space in spaces],
        out_specs=[pl.BlockSpec(memory_space=pltpu.VMEM)] * len(out),
        scratch_shapes=list(scratch),
        compiler_params=pltpu.CompilerParams(vmem_limit_bytes=limit * 2**20),
        cost_estimate=pl.CostEstimate(flops=1, bytes_accessed=cost, transcendentals=0),
        name=name,
    )(*held)


def power_kernel(wl_ref, spec_ref, notes_ref, own_ref, away_ref, wl_held, sems):
    row, col, core, *_ = place()
    n_col = lax.axis_size("col")
    _, parts, per, windows = spec_ref.shape
    wl_copy = pltpu.make_async_copy(wl_ref, wl_held, sems.at[2])
    wl_copy.start()
    both = ((core, own_ref), (1 - core, away_ref))
    copies = [pltpu.make_async_copy(spec_ref.at[f], held, sems.at[i]) for i, (f, held) in enumerate(both)]
    for copy in copies:
        copy.start()
    ids = (row * n_col + col) * per + lax.broadcasted_iota(jnp.int32, (1, per), 1)
    rest = jnp.zeros((notes_ref.shape[1] - per, LANES), jnp.float32)
    wl_copy.wait()
    for at, ((f, held), copy) in enumerate(zip(both, copies)):
        copy.wait()
        squares = jnp.square(held[...].astype(jnp.float32))
        squares = squares[0] + squares[1]
        squares = sum(squares[:, at : at + LANES] for at in range(0, windows, LANES))
        columns = jnp.transpose(jnp.concatenate([squares, rest], axis=0))
        power = jnp.sum(columns, axis=0, keepdims=True)
        level = jnp.sum(jnp.where(ids == wl_held[f], power[:, :per], 0.0), axis=1, keepdims=True)
        notes_ref[2 * at : 2 * at + 1, :] = power
        notes_ref[2 * at + 1 : 2 * at + 2, :] = jnp.broadcast_to(level, power.shape)


def gate_kernel(n, *refs):
    out_ref, start = refs[-1], 0
    for ref in refs[:n]:
        out_ref[start : start + ref.shape[0], :] = ref[...]
        start += ref.shape[0]


def gated(values, others):
    rows, width = sum(v.shape[0] for v in values), values[0].shape[1]
    return kernel_call(
        functools.partial(gate_kernel, len(values)),
        [vmem((rows, width), values[0].dtype)],
        [*values, *others],
        [pltpu.VMEM] * (len(values) + len(others)),
        name="gate",
    )[0]


def send_kernel(token_ref, own_ref, other_ref, to_x_ref, to_y_ref):
    y = place()[4]
    half = to_y_ref.shape[-1]
    theirs = pl.ds(pl.multiple_of((1 - y) * half, half), half)
    for at, ref in enumerate((own_ref, other_ref)):
        to_x_ref[at] = ref[...]
        for part in range(ref.shape[0]):
            to_y_ref[at, part] = ref[part, :, theirs]


def by_parity(values, block):
    width = values.shape[1]
    if 2 * block != LANES or width % (2 * LANES):
        order = [at for parity in (0, 1) for at in range(parity * block, width, 2 * block)]
        return jnp.concatenate([values[:, at : at + block] for at in order], axis=1)
    low = lax.broadcasted_iota(jnp.int32, (values.shape[0], LANES), 1) < block
    even, odd = [], []
    for at in range(0, width, 2 * LANES):
        first, second = values[:, at : at + LANES], values[:, at + LANES : at + 2 * LANES]
        even.append(jnp.where(low, first, pltpu.roll(second, block, 1)))
        odd.append(jnp.where(low, pltpu.roll(first, block, 1), second))
    return jnp.concatenate(even + odd, axis=1)


def steer_blocks(blocks, delays_ref, cos_ref, sin_ref, copy_ref=None, block=None):
    core = place()[2]
    rate = jnp.where(core == 0, cycle_rates[0], cycle_rates[1]).astype(jnp.float32)
    size = cos_ref.shape[0] // len(blocks)
    chunk = math.gcd(CHUNK, size)
    for index, (start, arrival) in enumerate(blocks):
        if arrival is not None:
            arrival.wait()

        @pl.loop(0, size // chunk, unroll=math.gcd(size // chunk, 10))
        def _(i):
            here = pl.ds(pl.multiple_of(start + i * chunk, chunk), chunk)
            there = pl.ds(pl.multiple_of(index * size + i * chunk, chunk), chunk)
            delays = delays_ref[here, :]
            if block:
                delays = by_parity(delays, block)
            cos, sin = steer_rows(rate, delays)
            cos_ref[there, :] = cos
            sin_ref[there, :] = sin
            if copy_ref is not None:
                copy_ref[there, :] = delays.astype(copy_ref.dtype)


def steer_kernel(token_ref, delays_ref, cos_ref, sin_ref, out_ref):
    out_ref[...] = token_ref[...]
    steer_blocks([(0, None)], delays_ref, cos_ref, sin_ref)


def steer_far_kernel(starts, parts, block, token_ref, delays_ref, cos_ref, sin_ref, out_ref, *refs):
    *copy_ref, held_ref, sems = refs
    out_ref[...] = token_ref[...]
    firsts = starts()
    per = cos_ref.shape[0] // len(firsts)
    rows = per // parts
    blocks = []
    for j, first in enumerate(firsts):
        for part in range(parts):
            index = j * parts + part
            here = pl.ds(index * rows, rows)
            there = pl.ds(pl.multiple_of(first + part * rows, 8), rows)
            arrival = pltpu.make_async_copy(delays_ref.at[there, :], held_ref.at[here, :], sems.at[index])
            arrival.start()
            blocks.append((index * rows, arrival))
    steer_blocks(blocks, held_ref, cos_ref, sin_ref, *(copy_ref or [None]), block)


def steering(token, delays):
    out = [vmem(delays.shape, jnp.bfloat16)] * 2 + [vmem(token.shape, token.dtype)]
    return kernel_call(steer_kernel, out, [token, delays], [pltpu.VMEM] * 2, name="steering")


def steering_far(starts, per, blocks, token, delays, copied=(), block=None):
    parts = math.gcd(per // CHUNK, 1 if block else 2)
    shape = (per * blocks, delays.shape[1])
    return kernel_call(
        functools.partial(steer_far_kernel, starts, parts, block),
        [vmem(shape, jnp.bfloat16)] * 2
        + [vmem(token.shape, token.dtype)]
        + [vmem(shape, t) for t in copied],
        [token, delays],
        [pltpu.VMEM, pltpu.HBM],
        scratch=[pltpu.VMEM(shape, delays.dtype), pltpu.SemaphoreType.DMA((blocks * parts,))],
        name="steering_far",
    )


def halves(total, block, bit, keep_ref, send_ref):
    for pair in range(keep_ref.shape[0] // block):
        out = pl.ds(pair * block, block)
        for ref, at in ((keep_ref, bit), (send_ref, 1 - bit)):
            rows = pl.ds(pl.multiple_of((2 * pair + at) * block, block), block)
            ref[out, :] = total[rows, :].astype(ref.dtype)


def beams_kernel(order, mine, block, kept, only, near_power_ref, far_ref, level_ref, own_ref, other_ref, from_ref, *refs):
    if only is None:
        *steer, keep_ref, send_ref, total_ref = refs
        beams_of = slice(None)
    else:
        *steer, total_ref = refs
        beams_of = pl.ds(pl.multiple_of(only() * total_ref.shape[0], total_ref.shape[0]), total_ref.shape[0])
    per = from_ref.shape[2]
    windows = mine(from_ref.shape[3])
    width = total_ref.shape[1] // 2
    powers = jnp.concatenate([near_power_ref[...], far_ref[:2]], axis=0)
    gains = lax.rsqrt(powers + 0.5 * level_ref[...])
    gains = jnp.transpose(jnp.concatenate([gains, gains], axis=0))[:per]
    scaled = []
    for at in range(4):
        near_ref = (own_ref, other_ref)[at % 2]
        spec = [near_ref[part, :, windows] if at < 2 else from_ref[at - 2, part] for part in (0, 1)]
        scaled.append(jnp.concatenate(spec, axis=1).astype(jnp.float32) * gains[:, at : at + 1])
    sums = [0.0, 0.0]
    for group, members in enumerate(order):
        right = jnp.concatenate([scaled[m] for m in members], axis=0).astype(jnp.bfloat16)
        for at in (0, 1):
            sums[at] += lax.dot_general(
                steer[2 * group + at][:, beams_of], right, (((0,), (0,)), ((), ())), preferred_element_type=jnp.float32
            )
    with_cos, with_sin = sums
    total_ref[:, :width] = (with_cos[:, :width] - with_sin[:, width:]).astype(total_ref.dtype)
    total_ref[:, width:] = (with_cos[:, width:] + with_sin[:, :width]).astype(total_ref.dtype)
    if only is None:
        halves(total_ref, block, kept(), keep_ref, send_ref)


def beams(order, mine, block, kept, near_power, far, level, own, other, arrived, steer, name, only=None, dtype=None):
    inputs = [near_power, far, level, own, other, arrived, *steer]
    rows, width = steer[0].shape[1], 2 * arrived.shape[-1]
    out = [vmem((rows // 2, width), t) for t in ((jnp.float32, jnp.bfloat16) if only is None else (dtype,))]
    return kernel_call(
        functools.partial(beams_kernel, order, mine, block, kept, only),
        out,
        inputs,
        [pltpu.VMEM] * len(inputs),
        scratch=[pltpu.VMEM((rows, width), jnp.float32)] if only is None else [],
        limit=24,
        name=name,
    )


def step_kernel(block, axis, bit, given, keep_ref, other_ref, token_ref, *outs):
    if given:
        *outs, out_token_ref = outs if bit is None else (*outs[:2], outs[3], outs[2])
        out_token_ref[...] = token_ref[...]
    if bit is None:
        total = keep_ref[...] + other_ref[...].astype(jnp.float32)
        for ref in outs:
            ref[...] = total.astype(ref.dtype)
    else:
        keep_out, send_out, total_ref = outs
        total_ref[...] = keep_ref[...] + other_ref[...].astype(jnp.float32)
        index = lax.axis_index(axis)
        halves(total_ref, block, (index // bit) & 1, keep_out, send_out)


def exchange(keep, send, block, steps, given, name):
    token = yield
    for index, (axis, bit, _) in enumerate(steps):
        other = swap(send, axis, bit)
        rows, width = keep.shape
        scratch, cut = [], (None, None)
        if index + 1 == len(steps):
            out = [vmem((rows, width), jnp.bfloat16)]
        elif steps[index + 1][2]:
            out, cut = [vmem((rows // 2, width), t) for t in (jnp.float32, jnp.bfloat16)], steps[index + 1][:2]
            scratch = [pltpu.VMEM((rows, width), jnp.float32)]
        else:
            out = [vmem((rows, width), t) for t in (jnp.float32, jnp.bfloat16)]
        if index in given:
            out.append(vmem(token.shape, token.dtype))
        results = kernel_call(
            functools.partial(step_kernel, block, *cut, index in given),
            out,
            [keep, other, token],
            [pltpu.VMEM] * 3,
            scratch=scratch,
            name=name,
        )
        if index + 1 == len(steps):
            yield results[0]
        else:
            keep, send = results[:2]
            token = yield results[-1]


def field_kernel(scale, mine, source_ref, near_r, far_r, field_ref):
    _, _, core, _, y = place()
    half = near_r.shape[1] // 2
    block = field_ref.shape[2]

    def product(left, right):
        return lax.dot_general(left, right, (((1,), (1,)), ((), ())), preferred_element_type=jnp.float32)

    rows = pl.ds(pl.multiple_of((core if mine else 1 - core) * block, block), block)
    real = imag = 0.0
    for bit, receiver in ((y, near_r), (1 - y, far_r)):
        s_re, s_im = (
            source_ref[:, pl.ds(pl.multiple_of((2 * part + bit) * half, half), half)] for part in (0, 1)
        )
        r_re, r_im = receiver[rows, :half], receiver[rows, half:]
        real += product(s_re, r_re) + product(s_im, r_im)
        imag += product(s_im, r_re) - product(s_re, r_im)
    field_ref[0] = real * scale
    field_ref[1] = imag * scale


def swap(value, axis, bit):
    size = lax.axis_size(axis)
    return lax.ppermute(value, axis, [(i, i ^ bit) for i in range(size)])


def choose(bit, first, second):
    return jnp.where(bit == 0, first, second)


def ordered(bit, own, other):
    return choose(bit, own, other), choose(bit, other, own)


def bits(size, start):
    found = []
    while start < size:
        found.append(start)
        start *= 2
    return found


def body(spectra, delays_s, delays_r, wl_index):
    n_row, n_col = lax.axis_size("row"), lax.axis_size("col")
    row, col, core, x, y = place()
    freqs, parts, per, windows = spectra.shape
    half = windows // 2
    padded = -(-per // LANES) * LANES

    spec_shape = vmem((parts, per, windows), spectra.dtype)
    block_r, block_s = 2 * delays_r.shape[1] // n_col, delays_s.shape[1] // n_row
    notes, own, away = kernel_call(
        power_kernel,
        [vmem((4, padded), jnp.float32), spec_shape, spec_shape],
        [wl_index, spectra],
        [pltpu.HBM, pltpu.HBM],
        scratch=[pltpu.SMEM(wl_index.shape, wl_index.dtype), pltpu.SemaphoreType.DMA((3,))],
        name="power",
    )
    other = swap(away, "col", 1)

    def starts_r():
        return [(place()[0] ^ j) * per for j in (0, 1)]

    def starts_s(first, last):
        return lambda: [block_of(j, at) * per for j, at in ((0, 0), (0, 1), (1, 0), (1, 1))[first:last]]

    far = swap(notes, "col", 2)
    *steer_r, token, near_r = steering_far(starts_r, per, 2, notes[:1], delays_r, [jnp.int16])
    other_r = swap(near_r, "col", 1)
    across = swap(gated([notes[2:], far[2:]], [token]), "col", 1)
    power, far_x = jnp.concatenate([notes[:1], across[:1]]), jnp.concatenate([far[:1], across[2:3]])
    level = (notes[1:2] + far[1:2]) + (across[1:2] + across[3:])

    sent = [vmem((2, parts, per, w), spectra.dtype) for w in (windows, half)]
    to_x, to_y = kernel_call(send_kernel, sent, [level, own, other], [pltpu.VMEM] * 3, name="send")
    from_x, from_y = swap(to_x, "col", 2), swap(to_y, "row", 1)

    row_bits, col_bits = bits(n_row, 2), bits(n_col, 4)
    first, *others = [("row", bit) for bit in row_bits[::-1]] + [("col", bit) for bit in col_bits]
    *steer_s, token = steering_far(starts_s(0, 2), per, 2, level, delays_s, block=block_s)
    level = level + swap(level, *first)
    cos, sin, next_token = steering_far(starts_s(2, 3), per, 1, level, delays_s, block=block_s)
    steer_s += [cos, sin]
    for step in others:
        level = gated([level], [token])
        level = level + swap(level, *step)
    cos, sin, token = steering(level, other_r)
    steer_r += [cos, sin]
    cos, sin, last_token = steering_far(starts_s(3, 4), per, 1, level, delays_s, block=block_s)
    steer_s += [cos, sin]
    far_y = swap(gated([power, level], [from_y, next_token]), "row", 1)
    level = gated([level + far_y[2:]], [token, last_token])

    keep_r, send_r = beams(
        ((0, 2), (1, 3)),
        lambda half: pl.ds(pl.multiple_of(y_of() * half, half), half),
        block_r,
        lambda: place()[3],
        power,
        far_y,
        level,
        own,
        other,
        from_y,
        steer_r,
        "beams_r",
    )
    (send_s,), (keep_s,) = (
        beams(
            ((0, 1), (2,), (3,)),
            lambda windows: slice(None),
            None,
            None,
            power,
            far_x,
            level,
            own,
            other,
            from_x,
            steer_s,
            "beams_s",
            only,
            dtype,
        )
        for only, dtype in ((lambda: 1 - y_of(), jnp.bfloat16), (y_of, jnp.float32))
    )
    r_steps = [("col", bit, True) for bit in [2, *col_bits]] + [("row", bit, False) for bit in row_bits]
    s_steps = [("row", bit, True) for bit in [1, *row_bits]] + [("col", bit, False) for bit in col_bits]
    late = 1
    r_chain = exchange(keep_r, send_r, block_r, r_steps, (), "step_r")
    s_chain = exchange(keep_s, send_s, block_s, s_steps, (late - 1,), "step_s")
    next(r_chain), next(s_chain)
    token = level
    for index in range(max(len(r_steps), len(s_steps))):
        if index < len(r_steps):
            receiver = r_chain.send(token if index == late else level)
        if index < len(s_steps):
            source = s_chain.send(level)
            if index == late - 1:
                token = source
    r_far = swap(receiver, "row", 1)

    block = delays_r.shape[1] // n_col
    shape = vmem((2, block_s, block), jnp.float32)
    scale = math.sqrt(windows) / (per * n_row * n_col)
    away, near = (
        kernel_call(
            functools.partial(field_kernel, scale, mine),
            [shape],
            [source, receiver, r_far],
            [pltpu.VMEM] * 3,
            name="field",
        )[0]
        for mine in (False, True)
    )
    far = swap(away, "col", 1)
    return jnp.stack(ordered(core, near, far)).swapaxes(2, 3)


def solution(mesh):
    in_specs = (P(None, None, ("row", "col"), None), P("row", None), P("col", None), P())
    out_specs = P(None, None, "col", "row")
    return jax.shard_map(body, mesh=mesh, in_specs=in_specs, out_specs=out_specs, check_vma=False)
```

```python
import functools
import math

import jax
import jax.numpy as jnp
from jax import lax
from jax.experimental import pallas as pl
from jax.experimental.pallas import tpu as pltpu
from jax.sharding import PartitionSpec as P

cycle_rates = (0.0361, 0.0596)
ROOT = math.sqrt(2.0)
SIN = (3.1415820121765137, -5.167142868041992, 2.5418989658355713, -0.5546361207962036)
COS = (0.9999999403953552, -4.934792995452881, 4.058412075042725, -1.3318800926208496, 0.2196967601776123)


def horner(z, terms):
    total = ROOT * terms[-1]
    for term in terms[-2::-1]:
        total = total * z + ROOT * term
    return total


def steer_rows(rate, delays):
    turns = rate * delays.astype(jnp.float32)
    turns = turns - jnp.round(turns)
    z = turns * turns
    half_sin = turns * horner(z, SIN)
    half_cos = horner(z, COS)
    return (1.0 - half_sin * half_sin).astype(jnp.bfloat16), (half_sin * half_cos).astype(jnp.bfloat16)


CHUNK = 32
LANES = 128


def place():
    row, col = lax.axis_index("row"), lax.axis_index("col")
    return row, col, col & 1, (col >> 1) & 1, row & 1


def y_of():
    return place()[4]


def block_of(j, at):
    _, col, core, x, _ = place()
    return (col >> 2) * 4 + (x ^ j) * 2 + (core ^ at)


def vmem(shape, dtype):
    return pltpu.VMEM(shape, dtype)


def kernel_call(body, out, inputs, spaces, scratch=(), limit=8, cost=1, name=None):
    held = [
        pltpu.with_memory_space_constraint(v, space) if space in (pltpu.HBM, pltpu.VMEM) else v
        for v, space in zip(inputs, spaces)
    ]
    return pl.pallas_call(
        body,
        out_shape=out,
        in_specs=[pl.BlockSpec(memory_space=space) for space in spaces],
        out_specs=[pl.BlockSpec(memory_space=pltpu.VMEM)] * len(out),
        scratch_shapes=list(scratch),
        compiler_params=pltpu.CompilerParams(vmem_limit_bytes=limit * 2**20),
        cost_estimate=pl.CostEstimate(flops=1, bytes_accessed=cost, transcendentals=0),
        name=name,
    )(*held)


def power_kernel(wl_ref, spec_ref, notes_ref, own_ref, away_ref, wl_held, sems):
    row, col, core, *_ = place()
    n_col = lax.axis_size("col")
    _, parts, per, windows = spec_ref.shape
    wl_copy = pltpu.make_async_copy(wl_ref, wl_held, sems.at[2])
    wl_copy.start()
    both = ((core, own_ref), (1 - core, away_ref))
    copies = [pltpu.make_async_copy(spec_ref.at[f], held, sems.at[i]) for i, (f, held) in enumerate(both)]
    for copy in copies:
        copy.start()
    ids = (row * n_col + col) * per + lax.broadcasted_iota(jnp.int32, (1, per), 1)
    rest = jnp.zeros((notes_ref.shape[1] - per, LANES), jnp.float32)
    wl_copy.wait()
    for at, ((f, held), copy) in enumerate(zip(both, copies)):
        copy.wait()
        squares = jnp.square(held[...].astype(jnp.float32))
        squares = squares[0] + squares[1]
        squares = sum(squares[:, at : at + LANES] for at in range(0, windows, LANES))
        columns = jnp.transpose(jnp.concatenate([squares, rest], axis=0))
        power = jnp.sum(columns, axis=0, keepdims=True)
        level = jnp.sum(jnp.where(ids == wl_held[f], power[:, :per], 0.0), axis=1, keepdims=True)
        notes_ref[2 * at : 2 * at + 1, :] = power
        notes_ref[2 * at + 1 : 2 * at + 2, :] = jnp.broadcast_to(level, power.shape)


def gate_kernel(n, *refs):
    out_ref, start = refs[-1], 0
    for ref in refs[:n]:
        out_ref[start : start + ref.shape[0], :] = ref[...]
        start += ref.shape[0]


def gated(values, others):
    rows, width = sum(v.shape[0] for v in values), values[0].shape[1]
    return kernel_call(
        functools.partial(gate_kernel, len(values)),
        [vmem((rows, width), values[0].dtype)],
        [*values, *others],
        [pltpu.VMEM] * (len(values) + len(others)),
        name="gate",
    )[0]


def send_kernel(token_ref, own_ref, other_ref, to_x_ref, to_y_ref):
    y = place()[4]
    half = to_y_ref.shape[-1]
    theirs = pl.ds(pl.multiple_of((1 - y) * half, half), half)
    for at, ref in enumerate((own_ref, other_ref)):
        to_x_ref[at] = ref[...]
        for part in range(ref.shape[0]):
            to_y_ref[at, part] = ref[part, :, theirs]


def by_parity(values, block):
    width = values.shape[1]
    if 2 * block != LANES or width % (2 * LANES):
        order = [at for parity in (0, 1) for at in range(parity * block, width, 2 * block)]
        return jnp.concatenate([values[:, at : at + block] for at in order], axis=1)
    low = lax.broadcasted_iota(jnp.int32, (values.shape[0], LANES), 1) < block
    even, odd = [], []
    for at in range(0, width, 2 * LANES):
        first, second = values[:, at : at + LANES], values[:, at + LANES : at + 2 * LANES]
        even.append(jnp.where(low, first, pltpu.roll(second, block, 1)))
        odd.append(jnp.where(low, pltpu.roll(first, block, 1), second))
    return jnp.concatenate(even + odd, axis=1)


def steer_blocks(blocks, delays_ref, cos_ref, sin_ref, copy_ref=None, block=None):
    core = place()[2]
    rate = jnp.where(core == 0, cycle_rates[0], cycle_rates[1]).astype(jnp.float32)
    size = cos_ref.shape[0] // len(blocks)
    chunk = math.gcd(CHUNK, size)
    for index, (start, arrival) in enumerate(blocks):
        if arrival is not None:
            arrival.wait()

        @pl.loop(0, size // chunk, unroll=math.gcd(size // chunk, 10))
        def _(i):
            here = pl.ds(pl.multiple_of(start + i * chunk, chunk), chunk)
            there = pl.ds(pl.multiple_of(index * size + i * chunk, chunk), chunk)
            delays = delays_ref[here, :]
            if block:
                delays = by_parity(delays, block)
            cos, sin = steer_rows(rate, delays)
            cos_ref[there, :] = cos
            sin_ref[there, :] = sin
            if copy_ref is not None:
                copy_ref[there, :] = delays.astype(copy_ref.dtype)


def steer_kernel(token_ref, *refs):
    *delays, cos_ref, sin_ref, out_ref = refs
    out_ref[...] = token_ref[...]
    rows = cos_ref.shape[0] // len(delays)
    for index, delays_ref in enumerate(delays):
        here = pl.ds(index * rows, rows)
        steer_blocks([(0, None)], delays_ref, cos_ref.at[here, :], sin_ref.at[here, :])


def steer_far_kernel(starts, parts, block, heads, token_ref, delays_ref, *refs):
    head, (cos_ref, sin_ref, out_ref, *copy_ref, held_ref, sems) = refs[:heads], refs[heads:]
    out_ref[...] = token_ref[...]
    firsts = starts()
    per = held_ref.shape[0] // len(firsts)
    rows = per // parts
    blocks = []
    for j, first in enumerate(firsts):
        for part in range(parts):
            index = j * parts + part
            here = pl.ds(index * rows, rows)
            there = pl.ds(pl.multiple_of(first + part * rows, 8), rows)
            arrival = pltpu.make_async_copy(delays_ref.at[there, :], held_ref.at[here, :], sems.at[index])
            arrival.start()
            blocks.append((index * rows, arrival))
    if head:
        above = head[0].shape[0]
        for ref, given in zip((cos_ref, sin_ref), head):
            ref[:above, :] = given[...]
        cos_ref, sin_ref = (ref.at[pl.ds(above, held_ref.shape[0]), :] for ref in (cos_ref, sin_ref))
    steer_blocks(blocks, held_ref, cos_ref, sin_ref, *(copy_ref or [None]), block)


def steering(token, delays):
    shape = (sum(d.shape[0] for d in delays), delays[0].shape[1])
    out = [vmem(shape, jnp.bfloat16)] * 2 + [vmem(token.shape, token.dtype)]
    inputs = [token, *delays]
    return kernel_call(steer_kernel, out, inputs, [pltpu.VMEM] * len(inputs), name="steering")


def steering_far(starts, per, blocks, token, delays, copied=(), block=None, head=()):
    parts = math.gcd(per // CHUNK, 1 if block else 2)
    shape = (per * blocks, delays.shape[1])
    whole = (shape[0] + (head[0].shape[0] if head else 0), shape[1])
    return kernel_call(
        functools.partial(steer_far_kernel, starts, parts, block, len(head)),
        [vmem(whole, jnp.bfloat16)] * 2
        + [vmem(token.shape, token.dtype)]
        + [vmem(shape, t) for t in copied],
        [token, delays, *head],
        [pltpu.VMEM, pltpu.HBM] + [pltpu.VMEM] * len(head),
        scratch=[pltpu.VMEM(shape, delays.dtype), pltpu.SemaphoreType.DMA((blocks * parts,))],
        name="steering_far",
    )


def halves(total, block, bit, keep_ref, send_ref):
    for pair in range(keep_ref.shape[0] // block):
        out = pl.ds(pair * block, block)
        for ref, at in ((keep_ref, bit), (send_ref, 1 - bit)):
            rows = pl.ds(pl.multiple_of((2 * pair + at) * block, block), block)
            ref[out, :] = total[rows, :].astype(ref.dtype)


def beams_kernel(order, mine, block, kept, only, near_power_ref, far_ref, level_ref, own_ref, other_ref, from_ref, *refs):
    if only is None:
        *steer, keep_ref, send_ref, token_ref, total_ref = refs
        token_ref[...] = level_ref[...]
        beams_of = slice(None)
    else:
        *steer, total_ref = refs
        beams_of = pl.ds(pl.multiple_of(only() * total_ref.shape[0], total_ref.shape[0]), total_ref.shape[0])
    per = from_ref.shape[2]
    windows = mine(from_ref.shape[3])
    width = total_ref.shape[1] // 2
    powers = jnp.concatenate([near_power_ref[...], far_ref[:2]], axis=0)
    gains = lax.rsqrt(powers + 0.5 * level_ref[...])
    gains = jnp.transpose(jnp.concatenate([gains, gains], axis=0))[:per]
    scaled = []
    for at in range(4):
        near_ref = (own_ref, other_ref)[at % 2]
        spec = [near_ref[part, :, windows] if at < 2 else from_ref[at - 2, part] for part in (0, 1)]
        scaled.append(jnp.concatenate(spec, axis=1).astype(jnp.float32) * gains[:, at : at + 1])
    sums = [0.0, 0.0]
    for group, members in enumerate(order):
        right = jnp.concatenate([scaled[m] for m in members], axis=0).astype(jnp.bfloat16)
        for at in (0, 1):
            sums[at] += lax.dot_general(
                steer[2 * group + at][:, beams_of], right, (((0,), (0,)), ((), ())), preferred_element_type=jnp.float32
            )
    with_cos, with_sin = sums
    total_ref[:, :width] = (with_cos[:, :width] - with_sin[:, width:]).astype(total_ref.dtype)
    total_ref[:, width:] = (with_cos[:, width:] + with_sin[:, :width]).astype(total_ref.dtype)
    if only is None:
        halves(total_ref, block, kept(), keep_ref, send_ref)


def beams(order, mine, block, kept, near_power, far, level, own, other, arrived, steer, name, only=None, dtype=None):
    inputs = [near_power, far, level, own, other, arrived, *steer]
    rows, width = steer[0].shape[1], 2 * arrived.shape[-1]
    out = [vmem((rows // 2, width), t) for t in ((jnp.float32, jnp.bfloat16) if only is None else (dtype,))]
    if only is None:
        out.append(vmem(level.shape, level.dtype))
    return kernel_call(
        functools.partial(beams_kernel, order, mine, block, kept, only),
        out,
        inputs,
        [pltpu.VMEM] * len(inputs),
        scratch=[pltpu.VMEM((rows, width), jnp.float32)] if only is None else [],
        limit=24,
        name=name,
    )


def step_kernel(block, axis, bit, given, keep_ref, other_ref, token_ref, *outs):
    if given:
        *outs, out_token_ref = outs if bit is None else (*outs[:2], outs[3], outs[2])
        out_token_ref[...] = token_ref[...]
    if bit is None:
        total = keep_ref[...] + other_ref[...].astype(jnp.float32)
        for ref in outs:
            ref[...] = total.astype(ref.dtype)
    else:
        keep_out, send_out, total_ref = outs
        total_ref[...] = keep_ref[...] + other_ref[...].astype(jnp.float32)
        index = lax.axis_index(axis)
        halves(total_ref, block, (index // bit) & 1, keep_out, send_out)


def exchange(keep, send, block, steps, given, name):
    token = yield
    for index, (axis, bit, _) in enumerate(steps):
        other = swap(send, axis, bit)
        rows, width = keep.shape
        scratch, cut = [], (None, None)
        if index + 1 == len(steps):
            out = [vmem((rows, width), jnp.bfloat16)]
        elif steps[index + 1][2]:
            out, cut = [vmem((rows // 2, width), t) for t in (jnp.float32, jnp.bfloat16)], steps[index + 1][:2]
            scratch = [pltpu.VMEM((rows, width), jnp.float32)]
        else:
            out = [vmem((rows, width), t) for t in (jnp.float32, jnp.bfloat16)]
        if index in given:
            out.append(vmem(token.shape, token.dtype))
        results = kernel_call(
            functools.partial(step_kernel, block, *cut, index in given),
            out,
            [keep, other, token],
            [pltpu.VMEM] * 3,
            scratch=scratch,
            name=name,
        )
        if index + 1 == len(steps):
            yield results[0]
        else:
            keep, send = results[:2]
            token = yield results[-1]


def field_kernel(scale, mine, source_ref, near_r, far_r, field_ref):
    _, _, core, _, y = place()
    half = near_r.shape[1] // 2
    block = field_ref.shape[2]

    def product(left, right):
        return lax.dot_general(left, right, (((1,), (1,)), ((), ())), preferred_element_type=jnp.float32)

    rows = pl.ds(pl.multiple_of((core if mine else 1 - core) * block, block), block)
    real = imag = 0.0
    for bit, receiver in ((y, near_r), (1 - y, far_r)):
        s_re, s_im = (
            source_ref[:, pl.ds(pl.multiple_of((2 * part + bit) * half, half), half)] for part in (0, 1)
        )
        r_re, r_im = receiver[rows, :half], receiver[rows, half:]
        real += product(s_re, r_re) + product(s_im, r_im)
        imag += product(s_im, r_re) - product(s_re, r_im)
    field_ref[0] = (real * scale).astype(field_ref.dtype)
    field_ref[1] = (imag * scale).astype(field_ref.dtype)


def swap(value, axis, bit):
    size = lax.axis_size(axis)
    return lax.ppermute(value, axis, [(i, i ^ bit) for i in range(size)])


def choose(bit, first, second):
    return jnp.where(bit == 0, first, second)


def ordered(bit, own, other):
    return choose(bit, own, other), choose(bit, other, own)


def bits(size, start):
    found = []
    while start < size:
        found.append(start)
        start *= 2
    return found


def body(spectra, delays_s, delays_r, wl_index):
    n_row, n_col = lax.axis_size("row"), lax.axis_size("col")
    row, col, core, x, y = place()
    freqs, parts, per, windows = spectra.shape
    half = windows // 2
    padded = -(-per // LANES) * LANES

    spec_shape = vmem((parts, per, windows), spectra.dtype)
    block_r, block_s = 2 * delays_r.shape[1] // n_col, delays_s.shape[1] // n_row
    notes, own, away = kernel_call(
        power_kernel,
        [vmem((4, padded), jnp.float32), spec_shape, spec_shape],
        [wl_index, spectra],
        [pltpu.HBM, pltpu.HBM],
        scratch=[pltpu.SMEM(wl_index.shape, wl_index.dtype), pltpu.SemaphoreType.DMA((3,))],
        name="power",
    )
    other = swap(away, "col", 1)

    def starts_r():
        return [(place()[0] ^ j) * per for j in (0, 1)]

    def starts_s(first, last):
        return lambda: [block_of(j, at) * per for j, at in ((0, 0), (0, 1), (1, 0), (1, 1))[first:last]]

    far = swap(notes, "col", 2)
    *steer_r, token, near_r = steering_far(starts_r, per, 2, notes[:1], delays_r, [jnp.int16])
    other_r = swap(near_r, "col", 1)
    across = swap(gated([notes[2:], far[2:]], [token]), "col", 1)
    power, far_x = jnp.concatenate([notes[:1], across[:1]]), jnp.concatenate([far[:1], across[2:3]])
    level = (notes[1:2] + far[1:2]) + (across[1:2] + across[3:])

    sent = [vmem((2, parts, per, w), spectra.dtype) for w in (windows, half)]
    to_x, to_y = kernel_call(send_kernel, sent, [level, own, other], [pltpu.VMEM] * 3, name="send")
    from_x, from_y = swap(to_x, "col", 2), swap(to_y, "row", 1)

    row_bits, col_bits = bits(n_row, 2), bits(n_col, 4)
    first, *others = [("row", bit) for bit in row_bits[::-1]] + [("col", bit) for bit in col_bits]
    *steer_s, token = steering_far(starts_s(0, 1), per, 1, level, delays_s, block=block_s)
    level = level + swap(level, *first)
    *steer_s, next_token = steering_far(starts_s(1, 2), per, 1, level, delays_s, block=block_s, head=steer_s)
    for step in others:
        level = gated([level], [token])
        level = level + swap(level, *step)
    cos, sin, token = steering(level, [other_r])
    steer_r += [cos, sin]
    *more_s, last_token = steering_far(starts_s(2, 3), per, 1, level, delays_s, block=block_s)
    far_y = swap(gated([power, level], [from_y, next_token]), "row", 1)
    level = gated([level + far_y[2:]], [token, last_token])

    keep_r, send_r, token = beams(
        ((0, 2), (1, 3)),
        lambda half: pl.ds(pl.multiple_of(y_of() * half, half), half),
        block_r,
        lambda: place()[3],
        power,
        far_y,
        level,
        own,
        other,
        from_y,
        steer_r,
        "beams_r",
    )
    steer_s += steering_far(starts_s(3, 4), per, 1, token, delays_s, block=block_s, head=more_s)[:2]
    (send_s,), (keep_s,) = (
        beams(
            ((0, 1), (2, 3)),
            lambda windows: slice(None),
            None,
            None,
            power,
            far_x,
            level,
            own,
            other,
            from_x,
            steer_s,
            "beams_s",
            only,
            dtype,
        )
        for only, dtype in ((lambda: 1 - y_of(), jnp.bfloat16), (y_of, jnp.float32))
    )
    r_steps = [("col", bit, True) for bit in [2, *col_bits]] + [("row", bit, False) for bit in row_bits]
    s_steps = [("row", bit, True) for bit in [1, *row_bits]] + [("col", bit, False) for bit in col_bits]
    late = 1
    r_chain = exchange(keep_r, send_r, block_r, r_steps, (), "step_r")
    s_chain = exchange(keep_s, send_s, block_s, s_steps, (late - 1,), "step_s")
    next(r_chain), next(s_chain)
    token = level
    for index in range(max(len(r_steps), len(s_steps))):
        if index < len(r_steps):
            receiver = r_chain.send(token if index == late else level)
        if index < len(s_steps):
            source = s_chain.send(level)
            if index == late - 1:
                token = source
    r_far = swap(receiver, "row", 1)

    block = delays_r.shape[1] // n_col
    scale = math.sqrt(windows) / (per * n_row * n_col)
    away, near = (
        kernel_call(
            functools.partial(field_kernel, scale, mine),
            [vmem((2, block_s, block), jnp.float32 if mine else jnp.bfloat16)],
            [source, receiver, r_far],
            [pltpu.VMEM] * 3,
            name="field",
        )[0]
        for mine in (False, True)
    )
    far = swap(away, "col", 1).astype(jnp.float32)
    return jnp.stack(ordered(core, near, far)).swapaxes(2, 3)


def solution(mesh):
    in_specs = (P(None, None, ("row", "col"), None), P("row", None), P("col", None), P())
    out_specs = P(None, None, "col", "row")
    return jax.shard_map(body, mesh=mesh, in_specs=in_specs, out_specs=out_specs, check_vma=False)
```

```python
import functools
import math

import jax
import jax.numpy as jnp
from jax import lax
from jax.experimental import pallas as pl
from jax.experimental.pallas import tpu as pltpu
from jax.sharding import PartitionSpec as P

cycle_rates = (0.0361, 0.0596)
ROOT = math.sqrt(2.0)
SIN = (3.1415820121765137, -5.167142868041992, 2.5418989658355713, -0.5546361207962036)
COS = (0.9999999403953552, -4.934792995452881, 4.058412075042725, -1.3318800926208496, 0.2196967601776123)


def horner(z, terms):
    total = ROOT * terms[-1]
    for term in terms[-2::-1]:
        total = total * z + ROOT * term
    return total


def steer_rows(rate, delays):
    turns = rate * delays.astype(jnp.float32)
    turns = turns - jnp.round(turns)
    z = turns * turns
    half_sin = turns * horner(z, SIN)
    half_cos = horner(z, COS)
    return (1.0 - half_sin * half_sin).astype(jnp.bfloat16), (half_sin * half_cos).astype(jnp.bfloat16)


CHUNK = 32
LANES = 128


def place():
    row, col = lax.axis_index("row"), lax.axis_index("col")
    return row, col, col & 1, (col >> 1) & 1, row & 1


def y_of():
    return place()[4]


def block_of(j, at):
    _, col, core, x, _ = place()
    return (col >> 2) * 4 + (x ^ j) * 2 + (core ^ at)


def vmem(shape, dtype):
    return pltpu.VMEM(shape, dtype)


def kernel_call(body, out, inputs, spaces, scratch=(), limit=8, cost=1, name=None):
    held = [
        pltpu.with_memory_space_constraint(v, space) if space in (pltpu.HBM, pltpu.VMEM) else v
        for v, space in zip(inputs, spaces)
    ]
    return pl.pallas_call(
        body,
        out_shape=out,
        in_specs=[pl.BlockSpec(memory_space=space) for space in spaces],
        out_specs=[pl.BlockSpec(memory_space=pltpu.VMEM)] * len(out),
        scratch_shapes=list(scratch),
        compiler_params=pltpu.CompilerParams(vmem_limit_bytes=limit * 2**20),
        cost_estimate=pl.CostEstimate(flops=1, bytes_accessed=cost, transcendentals=0),
        name=name,
    )(*held)


def power_kernel(wl_ref, spec_ref, notes_ref, own_ref, away_ref, wl_held, sems):
    row, col, core, *_ = place()
    n_col = lax.axis_size("col")
    _, parts, per, windows = spec_ref.shape
    wl_copy = pltpu.make_async_copy(wl_ref, wl_held, sems.at[2])
    wl_copy.start()
    both = ((core, own_ref), (1 - core, away_ref))
    copies = [pltpu.make_async_copy(spec_ref.at[f], held, sems.at[i]) for i, (f, held) in enumerate(both)]
    for copy in copies:
        copy.start()
    ids = (row * n_col + col) * per + lax.broadcasted_iota(jnp.int32, (1, per), 1)
    rest = jnp.zeros((notes_ref.shape[1] - per, LANES), jnp.float32)
    wl_copy.wait()
    for at, ((f, held), copy) in enumerate(zip(both, copies)):
        copy.wait()
        squares = jnp.square(held[...].astype(jnp.float32))
        squares = squares[0] + squares[1]
        squares = sum(squares[:, at : at + LANES] for at in range(0, windows, LANES))
        columns = jnp.transpose(jnp.concatenate([squares, rest], axis=0))
        power = jnp.sum(columns, axis=0, keepdims=True)
        level = jnp.sum(jnp.where(ids == wl_held[f], power[:, :per], 0.0), axis=1, keepdims=True)
        notes_ref[2 * at : 2 * at + 1, :] = power
        notes_ref[2 * at + 1 : 2 * at + 2, :] = jnp.broadcast_to(level, power.shape)


def gate_kernel(n, *refs):
    out_ref, start = refs[-1], 0
    for ref in refs[:n]:
        out_ref[start : start + ref.shape[0], :] = ref[...]
        start += ref.shape[0]


def gated(values, others):
    rows, width = sum(v.shape[0] for v in values), values[0].shape[1]
    return kernel_call(
        functools.partial(gate_kernel, len(values)),
        [vmem((rows, width), values[0].dtype)],
        [*values, *others],
        [pltpu.VMEM] * (len(values) + len(others)),
        name="gate",
    )[0]


def send_kernel(token_ref, own_ref, other_ref, to_x_ref, to_y_ref):
    y = place()[4]
    half = to_y_ref.shape[-1]
    theirs = pl.ds(pl.multiple_of((1 - y) * half, half), half)
    for at, ref in enumerate((own_ref, other_ref)):
        to_x_ref[at] = ref[...]
        for part in range(ref.shape[0]):
            to_y_ref[at, part] = ref[part, :, theirs]


def by_parity(values, block):
    width = values.shape[1]
    if 2 * block != LANES or width % (2 * LANES):
        order = [at for parity in (0, 1) for at in range(parity * block, width, 2 * block)]
        return jnp.concatenate([values[:, at : at + block] for at in order], axis=1)
    low = lax.broadcasted_iota(jnp.int32, (values.shape[0], LANES), 1) < block
    even, odd = [], []
    for at in range(0, width, 2 * LANES):
        first, second = values[:, at : at + LANES], values[:, at + LANES : at + 2 * LANES]
        even.append(jnp.where(low, first, pltpu.roll(second, block, 1)))
        odd.append(jnp.where(low, pltpu.roll(first, block, 1), second))
    return jnp.concatenate(even + odd, axis=1)


def steer_blocks(blocks, delays_ref, cos_ref, sin_ref, copy_ref=None, block=None):
    core = place()[2]
    rate = jnp.where(core == 0, cycle_rates[0], cycle_rates[1]).astype(jnp.float32)
    size = cos_ref.shape[0] // len(blocks)
    chunk = math.gcd(CHUNK, size)
    for index, (start, arrival) in enumerate(blocks):
        if arrival is not None:
            arrival.wait()

        @pl.loop(0, size // chunk, unroll=math.gcd(size // chunk, 10))
        def _(i):
            here = pl.ds(pl.multiple_of(start + i * chunk, chunk), chunk)
            there = pl.ds(pl.multiple_of(index * size + i * chunk, chunk), chunk)
            delays = delays_ref[here, :]
            if block:
                delays = by_parity(delays, block)
            cos, sin = steer_rows(rate, delays)
            cos_ref[there, :] = cos
            sin_ref[there, :] = sin
            if copy_ref is not None:
                copy_ref[there, :] = delays.astype(copy_ref.dtype)


def steer_kernel(token_ref, *refs):
    *delays, cos_ref, sin_ref, out_ref = refs
    out_ref[...] = token_ref[...]
    rows = cos_ref.shape[0] // len(delays)
    for index, delays_ref in enumerate(delays):
        here = pl.ds(index * rows, rows)
        steer_blocks([(0, None)], delays_ref, cos_ref.at[here, :], sin_ref.at[here, :])


def steer_far_kernel(starts, parts, block, heads, token_ref, delays_ref, *refs):
    head, (cos_ref, sin_ref, out_ref, *copy_ref, held_ref, sems) = refs[:heads], refs[heads:]
    out_ref[...] = token_ref[...]
    firsts = starts()
    per = held_ref.shape[0] // len(firsts)
    rows = per // parts
    blocks = []
    for j, first in enumerate(firsts):
        for part in range(parts):
            index = j * parts + part
            here = pl.ds(index * rows, rows)
            there = pl.ds(pl.multiple_of(first + part * rows, 8), rows)
            arrival = pltpu.make_async_copy(delays_ref.at[there, :], held_ref.at[here, :], sems.at[index])
            arrival.start()
            blocks.append((index * rows, arrival))
    if head:
        above = head[0].shape[0]
        for ref, given in zip((cos_ref, sin_ref), head):
            ref[:above, :] = given[...]
        cos_ref, sin_ref = (ref.at[pl.ds(above, held_ref.shape[0]), :] for ref in (cos_ref, sin_ref))
    steer_blocks(blocks, held_ref, cos_ref, sin_ref, *(copy_ref or [None]), block)


def steering(token, delays):
    shape = (sum(d.shape[0] for d in delays), delays[0].shape[1])
    out = [vmem(shape, jnp.bfloat16)] * 2 + [vmem(token.shape, token.dtype)]
    inputs = [token, *delays]
    return kernel_call(steer_kernel, out, inputs, [pltpu.VMEM] * len(inputs), name="steering")


def steering_far(starts, per, blocks, token, delays, copied=(), block=None, head=()):
    parts = 1
    shape = (per * blocks, delays.shape[1])
    whole = (shape[0] + (head[0].shape[0] if head else 0), shape[1])
    return kernel_call(
        functools.partial(steer_far_kernel, starts, parts, block, len(head)),
        [vmem(whole, jnp.bfloat16)] * 2
        + [vmem(token.shape, token.dtype)]
        + [vmem(shape, t) for t in copied],
        [token, delays, *head],
        [pltpu.VMEM, pltpu.HBM] + [pltpu.VMEM] * len(head),
        scratch=[pltpu.VMEM(shape, delays.dtype), pltpu.SemaphoreType.DMA((blocks * parts,))],
        name="steering_far",
    )


def halves(total, block, bit, keep_ref, send_ref):
    for pair in range(keep_ref.shape[0] // block):
        out = pl.ds(pair * block, block)
        for ref, at in ((keep_ref, bit), (send_ref, 1 - bit)):
            rows = pl.ds(pl.multiple_of((2 * pair + at) * block, block), block)
            ref[out, :] = total[rows, :].astype(ref.dtype)


def beams_kernel(order, mine, block, kept, only, near_power_ref, far_ref, level_ref, own_ref, other_ref, from_ref, *refs):
    if only is None:
        *steer, keep_ref, send_ref, token_ref, total_ref = refs
        token_ref[...] = level_ref[...]
        beams_of = slice(None)
    else:
        *steer, total_ref = refs
        beams_of = pl.ds(pl.multiple_of(only() * total_ref.shape[0], total_ref.shape[0]), total_ref.shape[0])
    per = from_ref.shape[2]
    windows = mine(from_ref.shape[3])
    width = total_ref.shape[1] // 2
    powers = jnp.concatenate([near_power_ref[...], far_ref[:2]], axis=0)
    gains = lax.rsqrt(powers + 0.5 * level_ref[...])
    gains = jnp.transpose(jnp.concatenate([gains, gains], axis=0))[:per]
    scaled = []
    for at in range(4):
        near_ref = (own_ref, other_ref)[at % 2]
        spec = [near_ref[part, :, windows] if at < 2 else from_ref[at - 2, part] for part in (0, 1)]
        scaled.append(jnp.concatenate(spec, axis=1).astype(jnp.float32) * gains[:, at : at + 1])
    sums = [0.0, 0.0]
    for group, members in enumerate(order):
        right = jnp.concatenate([scaled[m] for m in members], axis=0).astype(jnp.bfloat16)
        for at in (0, 1):
            sums[at] += lax.dot_general(
                steer[2 * group + at][:, beams_of], right, (((0,), (0,)), ((), ())), preferred_element_type=jnp.float32
            )
    with_cos, with_sin = sums
    total_ref[:, :width] = (with_cos[:, :width] - with_sin[:, width:]).astype(total_ref.dtype)
    total_ref[:, width:] = (with_cos[:, width:] + with_sin[:, :width]).astype(total_ref.dtype)
    if only is None:
        halves(total_ref, block, kept(), keep_ref, send_ref)


def beams(order, mine, block, kept, near_power, far, level, own, other, arrived, steer, name, only=None, dtype=None):
    inputs = [near_power, far, level, own, other, arrived, *steer]
    rows, width = steer[0].shape[1], 2 * arrived.shape[-1]
    out = [vmem((rows // 2, width), t) for t in ((jnp.float32, jnp.bfloat16) if only is None else (dtype,))]
    if only is None:
        out.append(vmem(level.shape, level.dtype))
    return kernel_call(
        functools.partial(beams_kernel, order, mine, block, kept, only),
        out,
        inputs,
        [pltpu.VMEM] * len(inputs),
        scratch=[pltpu.VMEM((rows, width), jnp.float32)] if only is None else [],
        limit=24,
        name=name,
    )


def step_kernel(block, axis, bit, given, keep_ref, other_ref, token_ref, *outs):
    if given:
        *outs, out_token_ref = outs if bit is None else (*outs[:2], outs[3], outs[2])
        out_token_ref[...] = token_ref[...]
    if bit is None:
        total = keep_ref[...] + other_ref[...].astype(jnp.float32)
        for ref in outs:
            ref[...] = total.astype(ref.dtype)
    else:
        keep_out, send_out, total_ref = outs
        total_ref[...] = keep_ref[...] + other_ref[...].astype(jnp.float32)
        index = lax.axis_index(axis)
        halves(total_ref, block, (index // bit) & 1, keep_out, send_out)


def exchange(keep, send, block, steps, given, name):
    token = yield
    for index, (axis, bit, _) in enumerate(steps):
        other = swap(send, axis, bit)
        rows, width = keep.shape
        scratch, cut = [], (None, None)
        if index + 1 == len(steps):
            out = [vmem((rows, width), jnp.bfloat16)]
        elif steps[index + 1][2]:
            out, cut = [vmem((rows // 2, width), t) for t in (jnp.float32, jnp.bfloat16)], steps[index + 1][:2]
            scratch = [pltpu.VMEM((rows, width), jnp.float32)]
        else:
            out = [vmem((rows, width), t) for t in (jnp.float32, jnp.bfloat16)]
        if index in given:
            out.append(vmem(token.shape, token.dtype))
        results = kernel_call(
            functools.partial(step_kernel, block, *cut, index in given),
            out,
            [keep, other, token],
            [pltpu.VMEM] * 3,
            scratch=scratch,
            name=name,
        )
        if index + 1 == len(steps):
            yield results[0]
        else:
            keep, send = results[:2]
            token = yield results[-1]


def field_kernel(scale, mine, source_ref, near_r, far_r, field_ref):
    _, _, core, _, y = place()
    half = near_r.shape[1] // 2
    block = field_ref.shape[2]

    def product(left, right):
        return lax.dot_general(left, right, (((1,), (1,)), ((), ())), preferred_element_type=jnp.float32)

    rows = pl.ds(pl.multiple_of((core if mine else 1 - core) * block, block), block)
    real = imag = 0.0
    for bit, receiver in ((y, near_r), (1 - y, far_r)):
        s_re, s_im = (
            source_ref[:, pl.ds(pl.multiple_of((2 * part + bit) * half, half), half)] for part in (0, 1)
        )
        r_re, r_im = receiver[rows, :half], receiver[rows, half:]
        real += product(s_re, r_re) + product(s_im, r_im)
        imag += product(s_im, r_re) - product(s_re, r_im)
    field_ref[0] = (real * scale).astype(field_ref.dtype)
    field_ref[1] = (imag * scale).astype(field_ref.dtype)


def swap(value, axis, bit):
    size = lax.axis_size(axis)
    return lax.ppermute(value, axis, [(i, i ^ bit) for i in range(size)])


def choose(bit, first, second):
    return jnp.where(bit == 0, first, second)


def ordered(bit, own, other):
    return choose(bit, own, other), choose(bit, other, own)


def bits(size, start):
    found = []
    while start < size:
        found.append(start)
        start *= 2
    return found


def body(spectra, delays_s, delays_r, wl_index):
    n_row, n_col = lax.axis_size("row"), lax.axis_size("col")
    row, col, core, x, y = place()
    freqs, parts, per, windows = spectra.shape
    half = windows // 2
    padded = -(-per // LANES) * LANES

    spec_shape = vmem((parts, per, windows), spectra.dtype)
    block_r, block_s = 2 * delays_r.shape[1] // n_col, delays_s.shape[1] // n_row
    notes, own, away = kernel_call(
        power_kernel,
        [vmem((4, padded), jnp.float32), spec_shape, spec_shape],
        [wl_index, spectra],
        [pltpu.HBM, pltpu.HBM],
        scratch=[pltpu.SMEM(wl_index.shape, wl_index.dtype), pltpu.SemaphoreType.DMA((3,))],
        name="power",
    )
    other = swap(away, "col", 1)

    def starts_r():
        return [(place()[0] ^ j) * per for j in (0, 1)]

    def starts_s(first, last):
        return lambda: [block_of(j, at) * per for j, at in ((0, 0), (0, 1), (1, 0), (1, 1))[first:last]]

    far = swap(notes, "col", 2)
    *steer_r, token, near_r = steering_far(starts_r, per, 2, notes[:1], delays_r, [jnp.int16])
    other_r = swap(near_r, "col", 1)
    across = swap(gated([notes[2:], far[2:]], [token]), "col", 1)
    power, far_x = jnp.concatenate([notes[:1], across[:1]]), jnp.concatenate([far[:1], across[2:3]])
    level = (notes[1:2] + far[1:2]) + (across[1:2] + across[3:])

    sent = [vmem((2, parts, per, w), spectra.dtype) for w in (windows, half)]
    to_x, to_y = kernel_call(send_kernel, sent, [level, own, other], [pltpu.VMEM] * 3, name="send")
    from_x, from_y = swap(to_x, "col", 2), swap(to_y, "row", 1)

    row_bits, col_bits = bits(n_row, 2), bits(n_col, 4)
    first, *others = [("row", bit) for bit in row_bits] + [("col", bit) for bit in col_bits]
    *steer_s, token = steering_far(starts_s(0, 1), per, 1, level, delays_s, block=block_s)
    level = level + swap(level, *first)
    *steer_s, next_token = steering_far(starts_s(1, 2), per, 1, level, delays_s, block=block_s, head=steer_s)
    for step in others:
        level = gated([level], [token])
        level = level + swap(level, *step)
    cos, sin, token = steering(level, [other_r])
    steer_r += [cos, sin]
    *more_s, last_token = steering_far(starts_s(2, 3), per, 1, level, delays_s, block=block_s)
    far_y = swap(gated([power, level], [from_y, next_token]), "row", 1)
    level = gated([level + far_y[2:]], [token, last_token])

    keep_r, send_r, token = beams(
        ((0, 2), (1, 3)),
        lambda half: pl.ds(pl.multiple_of(y_of() * half, half), half),
        block_r,
        lambda: place()[3],
        power,
        far_y,
        level,
        own,
        other,
        from_y,
        steer_r,
        "beams_r",
    )
    steer_s += steering_far(starts_s(3, 4), per, 1, token, delays_s, block=block_s, head=more_s)[:2]
    (send_s,), (keep_s,) = (
        beams(
            ((0, 1), (2, 3)),
            lambda windows: slice(None),
            None,
            None,
            power,
            far_x,
            level,
            own,
            other,
            from_x,
            steer_s,
            "beams_s",
            only,
            dtype,
        )
        for only, dtype in ((lambda: 1 - y_of(), jnp.bfloat16), (y_of, jnp.float32))
    )
    r_steps = [("col", bit, True) for bit in [2, *col_bits]] + [("row", bit, False) for bit in row_bits]
    s_steps = [("row", bit, True) for bit in [1, *row_bits]] + [("col", bit, False) for bit in col_bits]
    late = 1
    r_chain = exchange(keep_r, send_r, block_r, r_steps, (), "step_r")
    s_chain = exchange(keep_s, send_s, block_s, s_steps, (late - 1,), "step_s")
    next(r_chain), next(s_chain)
    token = level
    for index in range(max(len(r_steps), len(s_steps))):
        if index < len(r_steps):
            receiver = r_chain.send(token if index == late else level)
        if index < len(s_steps):
            source = s_chain.send(level)
            if index == late - 1:
                token = source
    r_far = swap(receiver, "row", 1)

    block = delays_r.shape[1] // n_col
    scale = math.sqrt(windows) / (per * n_row * n_col)
    away, near = (
        kernel_call(
            functools.partial(field_kernel, scale, mine),
            [vmem((2, block_s, block), jnp.float32 if mine else jnp.bfloat16)],
            [source, receiver, r_far],
            [pltpu.VMEM] * 3,
            name="field",
        )[0]
        for mine in (False, True)
    )
    far = swap(away, "col", 1).astype(jnp.float32)
    return jnp.stack(ordered(core, near, far)).swapaxes(2, 3)


def solution(mesh):
    in_specs = (P(None, None, ("row", "col"), None), P("row", None), P("col", None), P())
    out_specs = P(None, None, "col", "row")
    return jax.shard_map(body, mesh=mesh, in_specs=in_specs, out_specs=out_specs, check_vma=False)
```

```python
import functools
import math

import jax
import jax.numpy as jnp
from jax import lax
from jax.experimental import pallas as pl
from jax.experimental.pallas import tpu as pltpu
from jax.sharding import PartitionSpec as P

cycle_rates = (0.0361, 0.0596)
ROOT = math.sqrt(2.0)
SIN = (3.1415820121765137, -5.167142868041992, 2.5418989658355713, -0.5546361207962036)
COS = (0.9999999403953552, -4.934792995452881, 4.058412075042725, -1.3318800926208496, 0.2196967601776123)


def horner(z, terms):
    total = ROOT * terms[-1]
    for term in terms[-2::-1]:
        total = total * z + ROOT * term
    return total


def steer_rows(rate, delays):
    turns = rate * delays.astype(jnp.float32)
    turns = turns - jnp.round(turns)
    z = turns * turns
    half_sin = turns * horner(z, SIN)
    half_cos = horner(z, COS)
    return (1.0 - half_sin * half_sin).astype(jnp.bfloat16), (half_sin * half_cos).astype(jnp.bfloat16)


CHUNK = 32
LANES = 128


def place():
    row, col = lax.axis_index("row"), lax.axis_index("col")
    return row, col, col & 1, (col >> 1) & 1, row & 1


def y_of():
    return place()[4]


def block_of(j, at):
    _, col, core, x, _ = place()
    return (col >> 2) * 4 + (x ^ j) * 2 + (core ^ at)


def vmem(shape, dtype):
    return pltpu.VMEM(shape, dtype)


def kernel_call(body, out, inputs, spaces, scratch=(), limit=8, cost=1, name=None):
    held = [
        pltpu.with_memory_space_constraint(v, space) if space in (pltpu.HBM, pltpu.VMEM) else v
        for v, space in zip(inputs, spaces)
    ]
    return pl.pallas_call(
        body,
        out_shape=out,
        in_specs=[pl.BlockSpec(memory_space=space) for space in spaces],
        out_specs=[pl.BlockSpec(memory_space=pltpu.VMEM)] * len(out),
        scratch_shapes=list(scratch),
        compiler_params=pltpu.CompilerParams(vmem_limit_bytes=limit * 2**20),
        cost_estimate=pl.CostEstimate(flops=1, bytes_accessed=cost, transcendentals=0),
        name=name,
    )(*held)


def power_kernel(wl_ref, spec_ref, notes_ref, own_ref, away_ref, wl_held, sems):
    row, col, core, *_ = place()
    n_col = lax.axis_size("col")
    _, parts, per, windows = spec_ref.shape
    wl_copy = pltpu.make_async_copy(wl_ref, wl_held, sems.at[2])
    wl_copy.start()
    both = ((core, own_ref), (1 - core, away_ref))
    copies = [pltpu.make_async_copy(spec_ref.at[f], held, sems.at[i]) for i, (f, held) in enumerate(both)]
    for copy in copies:
        copy.start()
    ids = (row * n_col + col) * per + lax.broadcasted_iota(jnp.int32, (1, per), 1)
    rest = jnp.zeros((notes_ref.shape[1] - per, LANES), jnp.float32)
    wl_copy.wait()
    for at, ((f, held), copy) in enumerate(zip(both, copies)):
        copy.wait()
        squares = jnp.square(held[...].astype(jnp.float32))
        squares = squares[0] + squares[1]
        squares = sum(squares[:, at : at + LANES] for at in range(0, windows, LANES))
        columns = jnp.transpose(jnp.concatenate([squares, rest], axis=0))
        power = jnp.sum(columns, axis=0, keepdims=True)
        level = jnp.sum(jnp.where(ids == wl_held[f], power[:, :per], 0.0), axis=1, keepdims=True)
        notes_ref[2 * at : 2 * at + 1, :] = power
        notes_ref[2 * at + 1 : 2 * at + 2, :] = jnp.broadcast_to(level, power.shape)


def gate_kernel(n, *refs):
    out_ref, start = refs[-1], 0
    for ref in refs[:n]:
        out_ref[start : start + ref.shape[0], :] = ref[...]
        start += ref.shape[0]


def gated(values, others):
    rows, width = sum(v.shape[0] for v in values), values[0].shape[1]
    return kernel_call(
        functools.partial(gate_kernel, len(values)),
        [vmem((rows, width), values[0].dtype)],
        [*values, *others],
        [pltpu.VMEM] * (len(values) + len(others)),
        name="gate",
    )[0]


def send_kernel(token_ref, own_ref, other_ref, to_x_ref, to_y_ref):
    y = place()[4]
    half = to_y_ref.shape[-1]
    theirs = pl.ds(pl.multiple_of((1 - y) * half, half), half)
    for at, ref in enumerate((own_ref, other_ref)):
        to_x_ref[at] = ref[...]
        for part in range(ref.shape[0]):
            to_y_ref[at, part] = ref[part, :, theirs]


def by_parity(values, block):
    width = values.shape[1]
    if 2 * block != LANES or width % (2 * LANES):
        order = [at for parity in (0, 1) for at in range(parity * block, width, 2 * block)]
        return jnp.concatenate([values[:, at : at + block] for at in order], axis=1)
    low = lax.broadcasted_iota(jnp.int32, (values.shape[0], LANES), 1) < block
    even, odd = [], []
    for at in range(0, width, 2 * LANES):
        first, second = values[:, at : at + LANES], values[:, at + LANES : at + 2 * LANES]
        even.append(jnp.where(low, first, pltpu.roll(second, block, 1)))
        odd.append(jnp.where(low, pltpu.roll(first, block, 1), second))
    return jnp.concatenate(even + odd, axis=1)


def steer_blocks(blocks, delays_ref, cos_ref, sin_ref, copy_ref=None, block=None):
    core = place()[2]
    rate = jnp.where(core == 0, cycle_rates[0], cycle_rates[1]).astype(jnp.float32)
    size = cos_ref.shape[0] // len(blocks)
    chunk = math.gcd(CHUNK, size)
    for index, (start, arrival) in enumerate(blocks):
        if arrival is not None:
            arrival.wait()

        @pl.loop(0, size // chunk, unroll=math.gcd(size // chunk, 10))
        def _(i):
            here = pl.ds(pl.multiple_of(start + i * chunk, chunk), chunk)
            there = pl.ds(pl.multiple_of(index * size + i * chunk, chunk), chunk)
            delays = delays_ref[here, :]
            if block:
                delays = by_parity(delays, block)
            cos, sin = steer_rows(rate, delays)
            cos_ref[there, :] = cos
            sin_ref[there, :] = sin
            if copy_ref is not None:
                copy_ref[there, :] = delays.astype(copy_ref.dtype)


def steer_kernel(token_ref, *refs):
    *delays, cos_ref, sin_ref, out_ref = refs
    out_ref[...] = token_ref[...]
    rows = cos_ref.shape[0] // len(delays)
    for index, delays_ref in enumerate(delays):
        here = pl.ds(index * rows, rows)
        steer_blocks([(0, None)], delays_ref, cos_ref.at[here, :], sin_ref.at[here, :])


def steer_far_kernel(starts, parts, block, heads, token_ref, delays_ref, *refs):
    head, (cos_ref, sin_ref, out_ref, *copy_ref, held_ref, sems) = refs[:heads], refs[heads:]
    out_ref[...] = token_ref[...]
    firsts = starts()
    per = held_ref.shape[0] // len(firsts)
    rows = per // parts
    blocks = []
    for j, first in enumerate(firsts):
        for part in range(parts):
            index = j * parts + part
            here = pl.ds(index * rows, rows)
            there = pl.ds(pl.multiple_of(first + part * rows, 8), rows)
            arrival = pltpu.make_async_copy(delays_ref.at[there, :], held_ref.at[here, :], sems.at[index])
            arrival.start()
            blocks.append((index * rows, arrival))
    if head:
        above = head[0].shape[0]
        for ref, given in zip((cos_ref, sin_ref), head):
            ref[:above, :] = given[...]
        cos_ref, sin_ref = (ref.at[pl.ds(above, held_ref.shape[0]), :] for ref in (cos_ref, sin_ref))
    steer_blocks(blocks, held_ref, cos_ref, sin_ref, *(copy_ref or [None]), block)


def steering(token, delays):
    shape = (sum(d.shape[0] for d in delays), delays[0].shape[1])
    out = [vmem(shape, jnp.bfloat16)] * 2 + [vmem(token.shape, token.dtype)]
    inputs = [token, *delays]
    return kernel_call(steer_kernel, out, inputs, [pltpu.VMEM] * len(inputs), name="steering")


def steering_far(starts, per, blocks, token, delays, copied=(), block=None, head=()):
    parts = math.gcd(per // CHUNK, 1 if block else 2)
    shape = (per * blocks, delays.shape[1])
    whole = (shape[0] + (head[0].shape[0] if head else 0), shape[1])
    return kernel_call(
        functools.partial(steer_far_kernel, starts, parts, block, len(head)),
        [vmem(whole, jnp.bfloat16)] * 2
        + [vmem(token.shape, token.dtype)]
        + [vmem(shape, t) for t in copied],
        [token, delays, *head],
        [pltpu.VMEM, pltpu.HBM] + [pltpu.VMEM] * len(head),
        scratch=[pltpu.VMEM(shape, delays.dtype), pltpu.SemaphoreType.DMA((blocks * parts,))],
        name="steering_far",
    )


def halves(total, block, bit, keep_ref, send_ref):
    for pair in range(keep_ref.shape[0] // block):
        out = pl.ds(pair * block, block)
        for ref, at in ((keep_ref, bit), (send_ref, 1 - bit)):
            rows = pl.ds(pl.multiple_of((2 * pair + at) * block, block), block)
            ref[out, :] = total[rows, :].astype(ref.dtype)


def beams_kernel(order, mine, block, kept, only, near_power_ref, far_ref, level_ref, own_ref, other_ref, from_ref, *refs):
    if only is None:
        *steer, keep_ref, send_ref, token_ref, total_ref = refs
        token_ref[...] = level_ref[...]
        beams_of = slice(None)
    else:
        *steer, total_ref = refs
        beams_of = pl.ds(pl.multiple_of(only() * total_ref.shape[0], total_ref.shape[0]), total_ref.shape[0])
    per = from_ref.shape[2]
    windows = mine(from_ref.shape[3])
    width = total_ref.shape[1] // 2
    powers = jnp.concatenate([near_power_ref[...], far_ref[:2]], axis=0)
    gains = lax.rsqrt(powers + 0.5 * level_ref[...])
    gains = jnp.transpose(jnp.concatenate([gains, gains], axis=0))[:per]
    scaled = []
    for at in range(4):
        near_ref = (own_ref, other_ref)[at % 2]
        spec = [near_ref[part, :, windows] if at < 2 else from_ref[at - 2, part] for part in (0, 1)]
        scaled.append(jnp.concatenate(spec, axis=1).astype(jnp.float32) * gains[:, at : at + 1])
    sums = [0.0, 0.0]
    for group, members in enumerate(order):
        right = jnp.concatenate([scaled[m] for m in members], axis=0).astype(jnp.bfloat16)
        for at in (0, 1):
            sums[at] += lax.dot_general(
                steer[2 * group + at][:, beams_of], right, (((0,), (0,)), ((), ())), preferred_element_type=jnp.float32
            )
    with_cos, with_sin = sums
    total_ref[:, :width] = (with_cos[:, :width] - with_sin[:, width:]).astype(total_ref.dtype)
    total_ref[:, width:] = (with_cos[:, width:] + with_sin[:, :width]).astype(total_ref.dtype)
    if only is None:
        halves(total_ref, block, kept(), keep_ref, send_ref)


def beams(order, mine, block, kept, near_power, far, level, own, other, arrived, steer, name, only=None, dtype=None):
    inputs = [near_power, far, level, own, other, arrived, *steer]
    rows, width = steer[0].shape[1], 2 * arrived.shape[-1]
    out = [vmem((rows // 2, width), t) for t in ((jnp.float32, jnp.bfloat16) if only is None else (dtype,))]
    if only is None:
        out.append(vmem(level.shape, level.dtype))
    return kernel_call(
        functools.partial(beams_kernel, order, mine, block, kept, only),
        out,
        inputs,
        [pltpu.VMEM] * len(inputs),
        scratch=[pltpu.VMEM((rows, width), jnp.float32)] if only is None else [],
        limit=24,
        name=name,
    )


def step_kernel(block, axis, bit, given, keep_ref, other_ref, token_ref, *outs):
    if given:
        *outs, out_token_ref = outs if bit is None else (*outs[:2], outs[3], outs[2])
        out_token_ref[...] = token_ref[...]
    if bit is None:
        total = keep_ref[...] + other_ref[...].astype(jnp.float32)
        for ref in outs:
            ref[...] = total.astype(ref.dtype)
    else:
        keep_out, send_out, total_ref = outs
        total_ref[...] = keep_ref[...] + other_ref[...].astype(jnp.float32)
        index = lax.axis_index(axis)
        halves(total_ref, block, (index // bit) & 1, keep_out, send_out)


def exchange(keep, send, block, steps, given, name):
    token = yield
    for index, (axis, bit, _) in enumerate(steps):
        other = swap(send, axis, bit)
        rows, width = keep.shape
        scratch, cut = [], (None, None)
        if index + 1 == len(steps):
            out = [vmem((rows, width), jnp.bfloat16)]
        elif steps[index + 1][2]:
            out, cut = [vmem((rows // 2, width), t) for t in (jnp.float32, jnp.bfloat16)], steps[index + 1][:2]
            scratch = [pltpu.VMEM((rows, width), jnp.float32)]
        else:
            out = [vmem((rows, width), t) for t in (jnp.float32, jnp.bfloat16)]
        if index in given:
            out.append(vmem(token.shape, token.dtype))
        results = kernel_call(
            functools.partial(step_kernel, block, *cut, index in given),
            out,
            [keep, other, token],
            [pltpu.VMEM] * 3,
            scratch=scratch,
            name=name,
        )
        if index + 1 == len(steps):
            yield results[0]
        else:
            keep, send = results[:2]
            token = yield results[-1]


def field_kernel(scale, mine, source_ref, near_r, far_r, field_ref):
    _, _, core, _, y = place()
    half = near_r.shape[1] // 2
    block = field_ref.shape[2]

    def product(left, right):
        return lax.dot_general(left, right, (((1,), (1,)), ((), ())), preferred_element_type=jnp.float32)

    rows = pl.ds(pl.multiple_of((core if mine else 1 - core) * block, block), block)
    real = imag = 0.0
    for bit, receiver in ((y, near_r), (1 - y, far_r)):
        s_re, s_im = (
            source_ref[:, pl.ds(pl.multiple_of((2 * part + bit) * half, half), half)] for part in (0, 1)
        )
        r_re, r_im = receiver[rows, :half], receiver[rows, half:]
        real += product(s_re, r_re) + product(s_im, r_im)
        imag += product(s_im, r_re) - product(s_re, r_im)
    field_ref[0] = (real * scale).astype(field_ref.dtype)
    field_ref[1] = (imag * scale).astype(field_ref.dtype)


def swap(value, axis, bit):
    size = lax.axis_size(axis)
    return lax.ppermute(value, axis, [(i, i ^ bit) for i in range(size)])


def choose(bit, first, second):
    return jnp.where(bit == 0, first, second)


def ordered(bit, own, other):
    return choose(bit, own, other), choose(bit, other, own)


def bits(size, start):
    found = []
    while start < size:
        found.append(start)
        start *= 2
    return found


def body(spectra, delays_s, delays_r, wl_index):
    n_row, n_col = lax.axis_size("row"), lax.axis_size("col")
    row, col, core, x, y = place()
    freqs, parts, per, windows = spectra.shape
    half = windows // 2
    padded = -(-per // LANES) * LANES

    spec_shape = vmem((parts, per, windows), spectra.dtype)
    block_r, block_s = 2 * delays_r.shape[1] // n_col, delays_s.shape[1] // n_row
    notes, own, away = kernel_call(
        power_kernel,
        [vmem((4, padded), jnp.float32), spec_shape, spec_shape],
        [wl_index, spectra],
        [pltpu.HBM, pltpu.HBM],
        scratch=[pltpu.SMEM(wl_index.shape, wl_index.dtype), pltpu.SemaphoreType.DMA((3,))],
        name="power",
    )
    other = swap(away, "col", 1)

    def starts_r():
        return [(place()[0] ^ j) * per for j in (0, 1)]

    def starts_s(first, last):
        return lambda: [block_of(j, at) * per for j, at in ((0, 0), (0, 1), (1, 0), (1, 1))[first:last]]

    far = swap(notes, "col", 2)
    *steer_r, token, near_r = steering_far(starts_r, per, 2, notes[:1], delays_r, [jnp.int16])
    other_r = swap(near_r, "col", 1)
    across = swap(gated([notes[2:], far[2:]], [token]), "col", 1)
    power, far_x = jnp.concatenate([notes[:1], across[:1]]), jnp.concatenate([far[:1], across[2:3]])
    level = (notes[1:2] + far[1:2]) + (across[1:2] + across[3:])

    sent = [vmem((2, parts, per, w), spectra.dtype) for w in (windows, half)]
    to_x, to_y = kernel_call(send_kernel, sent, [level, own, other], [pltpu.VMEM] * 3, name="send")
    from_x, from_y = swap(to_x, "col", 2), swap(to_y, "row", 1)

    row_bits, col_bits = bits(n_row, 2), bits(n_col, 4)
    first, *others = [("row", bit) for bit in row_bits] + [("col", bit) for bit in col_bits]
    *steer_s, token = steering_far(starts_s(0, 1), per, 1, level, delays_s, block=block_s)
    level = level + swap(level, *first)
    *steer_s, next_token = steering_far(starts_s(1, 2), per, 1, level, delays_s, block=block_s, head=steer_s)
    for step in others:
        level = gated([level], [token])
        level = level + swap(level, *step)
    cos, sin, token = steering(level, [other_r])
    steer_r += [cos, sin]
    *more_s, last_token = steering_far(starts_s(2, 3), per, 1, level, delays_s, block=block_s)
    far_y = swap(gated([power, level], [from_y, next_token]), "row", 1)
    level = gated([level + far_y[2:]], [token, last_token])

    keep_r, send_r, token = beams(
        ((0, 2), (1, 3)),
        lambda half: pl.ds(pl.multiple_of(y_of() * half, half), half),
        block_r,
        lambda: place()[3],
        power,
        far_y,
        level,
        own,
        other,
        from_y,
        steer_r,
        "beams_r",
    )
    steer_s += steering_far(starts_s(3, 4), per, 1, token, delays_s, block=block_s, head=more_s)[:2]
    (send_s,), (keep_s,) = (
        beams(
            ((0, 1), (2, 3)),
            lambda windows: slice(None),
            None,
            None,
            power,
            far_x,
            level,
            own,
            other,
            from_x,
            steer_s,
            "beams_s",
            only,
            dtype,
        )
        for only, dtype in ((lambda: 1 - y_of(), jnp.bfloat16), (y_of, jnp.float32))
    )
    r_steps = [("col", bit, True) for bit in [2, *col_bits]] + [("row", bit, False) for bit in row_bits]
    s_steps = [("row", bit, True) for bit in [1, *row_bits]] + [("col", bit, False) for bit in col_bits]
    late = 1
    r_chain = exchange(keep_r, send_r, block_r, r_steps, (), "step_r")
    s_chain = exchange(keep_s, send_s, block_s, s_steps, (late - 1,), "step_s")
    next(r_chain), next(s_chain)
    token = level
    for index in range(max(len(r_steps), len(s_steps))):
        if index < len(r_steps):
            receiver = r_chain.send(token if index == late else level)
        if index < len(s_steps):
            source = s_chain.send(level)
            if index == late - 1:
                token = source
    r_far = swap(receiver, "row", 1)

    block = delays_r.shape[1] // n_col
    scale = math.sqrt(windows) / (per * n_row * n_col)
    away, near = (
        kernel_call(
            functools.partial(field_kernel, scale, mine),
            [vmem((2, block_s, block), jnp.float32 if mine else jnp.bfloat16)],
            [source, receiver, r_far],
            [pltpu.VMEM] * 3,
            name="field",
        )[0]
        for mine in (False, True)
    )
    far = swap(away, "col", 1).astype(jnp.float32)
    return jnp.stack(ordered(core, near, far)).swapaxes(2, 3)


def solution(mesh):
    in_specs = (P(None, None, ("row", "col"), None), P("row", None), P("col", None), P())
    out_specs = P(None, None, "col", "row")
    return jax.shard_map(body, mesh=mesh, in_specs=in_specs, out_specs=out_specs, check_vma=False)
```
